128 devices in a mesh: dev: 128 (over z, x, y, core).
Axes of the slice: x: 4, y: 4, z: 4, core: 2. Of those that a mesh axis runs over, the one named last changes fastest.
Arguments:
- lambda0: float32 [10, 7, 7, 65536], P(None, None, None, 'dev'), may hold values from -6 to 6
- order: int32 [65536], P('dev'), may hold values from 3 to 6
- send_index: int32 [128, 512], P('dev'), may hold values from 0 to 511, each once within a row
- recv_slot: int32 [128, 512], P('dev'), may hold values from 0 to 511, each once within a row
- objective_grad: float32 [10, 7, 7, 65536], P(None, None, None, 'dev'), may hold values from -6 to 6
- metric: float32 [2, 65536], P(None, 'dev'), may hold values from 0.03 to 0.1
- pseudo_step: float32 [65536], P('dev'), may hold values from 0.05 to 0.25
- couplings: float32 [4, 10, 10], replicated, may hold values from -1.25 to 1.25
- neighbour: int32 [4, 65536], P(None, 'dev'), may hold values from 0 to 1023, as said below
- neighbour_face: int32 [4, 65536], P(None, 'dev'), may hold values from 0 to 3
- orient: int32 [4, 65536], P(None, 'dev'), may hold values from 0 to 1
- halo_send: int32 [2, 32768], P(None, 'dev'), may hold values from 0 to 511, as said below
Outputs:
- adjoint_two: float32 [10, 7, 7, 65536], P(None, None, None, 'dev')
- residual_one: float32 [10, 7, 7, 65536], P(None, None, None, 'dev')
The draws below stay inside these ranges and needn't reach their ends.
Inputs may be any that keep to these rules, and one draw needn't show every extreme that they name: `send_index`: each row is a permutation of 0 to 511. `recv_slot`: each row is a permutation of 0 to 511. `neighbour`: values 512 + x name position x of the below owner's last-row list, 768 + x position x of the above owner's first-row list; each ghost is named once. `halo_send`: each owner's two lists hold 256 distinct local slots each, slots of that owner.
All inputs are finite; a program needn't handle non-finite values.
Results may differ from the reference program's by a relative error of at most 0.00007.
Values sent between devices are 32-bit elements; how exact they have to be, the bound alone decides.
A program may use at most 128 MiB of HBM per device.

```python
import math
import jax
import jax.numpy as jnp
from jax import lax

F = 10
P_SIZE = 7
GX = 256
ROWS = 2
E_DEV = 512
CAP = 4
ELEMS = 65536
N_DEV = 128


def mesh_lists(key):
    key_perm, key_rot = jax.random.split(key)
    slot_of_cell = jax.vmap(lambda sub: jax.random.permutation(sub, E_DEV))(jax.random.split(key_perm, N_DEV)).astype(jnp.int32)
    rotation = jax.random.randint(key_rot, (N_DEV, E_DEV), 0, 4).astype(jnp.int32)
    cell = jnp.arange(E_DEV, dtype=jnp.int32)[None, :]
    device = jnp.arange(N_DEV, dtype=jnp.int32)[:, None]
    column = cell % GX
    global_row = device * ROWS + cell // GX
    all_rows = N_DEV * ROWS
    own_slot = jnp.broadcast_to(slot_of_cell, (N_DEV, E_DEV))
    device_full = jnp.broadcast_to(device, (N_DEV, E_DEV))
    across_out = jnp.zeros((4, N_DEV, E_DEV), jnp.int32)
    face_out = jnp.zeros((4, N_DEV, E_DEV), jnp.int32)
    orient_out = jnp.zeros((4, N_DEV, E_DEV), jnp.int32)
    row_steps = [-1, 0, 1, 0]
    col_steps = [0, 1, 0, -1]
    for direction in range(4):
        next_row = (global_row + row_steps[direction]) % all_rows
        next_col = (column + col_steps[direction]) % GX
        next_dev = next_row // ROWS
        next_cell = next_row % ROWS * GX + next_col
        next_slot = slot_of_cell[next_dev, next_cell]
        next_rot = rotation[next_dev, next_cell]
        own_face = (direction - rotation) % 4
        back_face = (direction + 2 - next_rot) % 4
        own_along = jnp.where(own_face % 2 == 0, 1 + rotation, 2 + rotation) % 4
        back_along = jnp.where(back_face % 2 == 0, 1 + next_rot, 2 + next_rot) % 4
        flipped = ((own_along - back_along) % 4 == 2).astype(jnp.int32)
        if direction == 0:
            ghost = E_DEV + next_col
        else:
            ghost = E_DEV + GX + next_col
        target = jnp.where(next_dev == device, next_slot, ghost).astype(jnp.int32)
        across_out = across_out.at[own_face, device_full, own_slot].set(target)
        face_out = face_out.at[own_face, device_full, own_slot].set(back_face.astype(jnp.int32))
        orient_out = orient_out.at[own_face, device_full, own_slot].set(flipped)
    bottom_row = slot_of_cell[:, :GX]
    top_row = slot_of_cell[:, (ROWS - 1) * GX:]
    sends = jnp.stack([bottom_row, top_row], axis=0).reshape(2, N_DEV * GX)
    return (across_out.reshape(4, N_DEV * E_DEV), face_out.reshape(4, N_DEV * E_DEV), orient_out.reshape(4, N_DEV * E_DEV), sends)


def draw_neighbour(key, part):
    return mesh_lists(key)[0]


def draw_neighbour_face(key, part):
    return mesh_lists(key)[1]


def draw_orient(key, part):
    return mesh_lists(key)[2]


def draw_halo_send(key, part):
    return mesh_lists(key)[3]


def touch_ends(array, key, low, high):
    spot = [jax.random.randint(jax.random.fold_in(key, axis), (), 0, length) for axis, length in enumerate(array.shape)]
    main_axis = array.shape.index(max(array.shape))
    next_to = spot[:main_axis] + [(spot[main_axis] + 1) % array.shape[main_axis]] + spot[main_axis + 1:]
    return array.at[tuple(spot)].set(low).at[tuple(next_to)].set(high)


def level_of(rng, dims, pieces, smallest, high):
    def one(axis_at, parts):
        heights = jax.random.uniform(jax.random.fold_in(jax.random.fold_in(rng, 6), axis_at), (parts,), jnp.float32, smallest / len(pieces), high / len(pieces))
        return jnp.repeat(jnp.exp(heights), dims[axis_at] // parts).reshape((-1,) + (1,) * (len(dims) - axis_at - 1))

    factor_of = one(*pieces[0])
    for cut in pieces[1:]:
        factor_of = factor_of * one(*cut)
    return factor_of


def scatter_about(own_key, shape, spread, bound, shards=(), kind=jnp.bfloat16):
    values = spread * jax.random.normal(own_key, shape, jnp.float32)
    if shards:
        values = values * level_of(own_key, shape, shards, -0.22, 0.18)
    return jnp.clip(values, -bound, bound).astype(kind)


def setup_inputs(seed: int = 0) -> dict:
    streams_of = jax.random.split(jax.random.key(seed), 13)
    return {
        "lambda0": scatter_about(streams_of[0], (F, P_SIZE, P_SIZE, ELEMS), 1.0, 6.0, ((3, 128),), jnp.float32),
        "order": touch_ends(jax.random.randint(streams_of[1], (ELEMS,), 3, 7), jax.random.fold_in(streams_of[1], 1), 3, 6).astype(jnp.int32),
        "send_index": jax.vmap(lambda own: jax.random.permutation(own, E_DEV))(jax.random.split(streams_of[2], N_DEV)).reshape((N_DEV, E_DEV)).astype(jnp.int32),
        "recv_slot": jax.vmap(lambda own: jax.random.permutation(own, E_DEV))(jax.random.split(streams_of[3], N_DEV)).reshape((N_DEV, E_DEV)).astype(jnp.int32),
        "objective_grad": scatter_about(streams_of[4], (F, P_SIZE, P_SIZE, ELEMS), 1.0, 6.0, ((3, 128),), jnp.float32),
        "metric": jnp.clip(jnp.exp(math.log(0.1) - 1.2039728 * jax.random.uniform(streams_of[5], (2, ELEMS), jnp.float32) ** level_of(streams_of[5], (2, ELEMS), ((1, 128),), -0.2, 0.2)), 0.03, 0.1),
        "pseudo_step": jnp.clip(jnp.exp(math.log(0.25) - 1.609438 * jax.random.uniform(streams_of[6], (ELEMS,), jnp.float32) ** level_of(streams_of[6], (ELEMS,), ((0, 128),), -0.2, 0.2)), 0.05, 0.25),
        "couplings": scatter_about(streams_of[7], (4, F, F), (2 * F) ** -0.5, 1.25, (), jnp.float32),
        "neighbour": draw_neighbour(jax.random.fold_in(streams_of[12], 71), 0),
        "neighbour_face": draw_neighbour_face(jax.random.fold_in(streams_of[12], 71), 0),
        "orient": draw_orient(jax.random.fold_in(streams_of[12], 71), 0),
        "halo_send": draw_halo_send(jax.random.fold_in(streams_of[12], 71), 0),
    }


def basis_tables(size):
    mode_index = jnp.arange(size, dtype=jnp.int32)
    parity = jnp.where(mode_index % 2 == 0, 1.0, -1.0).astype(jnp.float32)
    lower = mode_index[:, None]
    upper = mode_index[None, :]
    derivative = jnp.where((lower < upper) & ((lower + upper) % 2 == 1), (2 * lower + 1).astype(jnp.float32), 0.0).astype(jnp.float32)
    return parity, derivative


def face_traces(field, parity):
    face_south = jnp.einsum('fije,j->fie', field, parity, precision=lax.Precision.HIGHEST)
    face_east = jnp.sum(field, axis=1)
    face_north = jnp.sum(field, axis=2)
    face_west = jnp.einsum('fije,i->fje', field, parity, precision=lax.Precision.HIGHEST)
    return jnp.stack([face_south, face_east, face_north, face_west], axis=2)


def volume_term(field, derivative, couplings, metric):
    grad_x = jnp.einsum('ai,gaje->gije', derivative, field, precision=lax.Precision.HIGHEST)
    grad_y = jnp.einsum('bj,gibe->gije', derivative, field, precision=lax.Precision.HIGHEST)
    mixed_x = jnp.einsum('gf,gije->fije', couplings[0], grad_x, precision=lax.Precision.HIGHEST)
    mixed_y = jnp.einsum('gf,gije->fije', couplings[1], grad_y, precision=lax.Precision.HIGHEST)
    reaction = jnp.einsum('gf,gije->fije', couplings[2], field, precision=lax.Precision.HIGHEST)
    return metric[0] * mixed_x + metric[1] * mixed_y + reaction


def lift_faces(traces, facing, orient, couplings, parity):
    flip = jnp.where(orient[None, :, :] == 1, parity[:, None, None], 1.0).astype(jnp.float32)
    jump = traces - facing * flip[None]
    flux = jnp.einsum('gf,gmke->fmke', couplings[3], jump, precision=lax.Precision.HIGHEST)
    lifted = flux[:, :, 0, None, :] * parity[None, None, :, None] + flux[:, :, 2, None, :]
    lifted = lifted + flux[:, :, 1, :][:, None, :, :]
    lifted = lifted + parity[None, :, None, None] * flux[:, :, 3, :][:, None, :, :]
    return lifted


def reference(lambda0, order, send_index, recv_slot, objective_grad, metric, pseudo_step, couplings, neighbour, neighbour_face, orient, halo_send):
    position = jnp.arange(E_DEV, dtype=jnp.int32)
    target = position // CAP
    within = position % CAP
    source = jnp.arange(N_DEV, dtype=jnp.int32)[:, None]
    old_global = (source * E_DEV + send_index).reshape(-1)
    new_global = (target[None, :] * E_DEV + recv_slot[target[None, :], source * CAP + within[None, :]]).reshape(-1)
    moved = jnp.zeros_like(lambda0).at[:, :, :, new_global].set(lambda0[:, :, :, old_global])
    order_moved = jnp.zeros((ELEMS,), jnp.int32).at[new_global].set(order[old_global])
    mode_index = jnp.arange(P_SIZE, dtype=jnp.int32)
    mask = ((mode_index[:, None, None] <= order_moved[None, None, :]) & (mode_index[None, :, None] <= order_moved[None, None, :])).astype(jnp.float32)
    parity, derivative = basis_tables(P_SIZE)
    element = jnp.arange(ELEMS, dtype=jnp.int32)
    owner = (element // E_DEV)[None, :]
    below = (owner - 1) % N_DEV
    above = (owner + 1) % N_DEV
    from_below = jnp.clip(neighbour - E_DEV, 0, GX - 1)
    from_above = jnp.clip(neighbour - E_DEV - GX, 0, GX - 1)
    ghost_below = below * E_DEV + halo_send[1][below * GX + from_below]
    ghost_above = above * E_DEV + halo_send[0][above * GX + from_above]
    across = jnp.where(neighbour < E_DEV, owner * E_DEV + neighbour, jnp.where(neighbour < E_DEV + GX, ghost_below, ghost_above))

    def residual(field):
        traces = face_traces(field, parity)
        facing = traces[:, :, neighbour_face, across]
        lifted = lift_faces(traces, facing, orient, couplings, parity)
        volume = volume_term(field, derivative, couplings, metric)
        return mask * (volume + lifted - objective_grad)

    adjoint_zero = mask * moved
    residual_zero = residual(adjoint_zero)
    adjoint_one = adjoint_zero - pseudo_step * residual_zero
    residual_one = residual(adjoint_one)
    adjoint_two = adjoint_one - pseudo_step * residual_one
    return adjoint_two, residual_one
```

```python
import functools

import jax
import jax.numpy as jnp
from jax import lax
from jax.experimental import pallas as pl
from jax.experimental.pallas import tpu as pltpu
from jax.sharding import PartitionSpec as P

F = 10
M = 7
E = 512
HALO = 256
PLACE = (0, 2, 4, 6, 1, 3, 5)
EVEN = (0, 2, 4, 6)
ODD = (1, 3, 5)
BLOCK = 8 * F
ROWS = M * BLOCK
NN = (((1,), (0,)), ((), ()))
NT = (((1,), (1,)), ((), ()))
F32 = jnp.float32
BF16 = jnp.bfloat16


def iota(shape, dim):
    return lax.broadcasted_iota(jnp.int32, shape, dim)


def dot(a, b, dims=NN):
    return lax.dot_general(a, b, dims, preferred_element_type=F32)


def exact_dot(a, b, dims=NN):
    return lax.dot_general(
        a, b, dims, precision=lax.Precision.HIGHEST, preferred_element_type=F32
    )


def halves(value):
    high = value.astype(BF16)
    low = (value - high.astype(F32)).astype(BF16)
    return high, low


def one_hot(equal):
    return jnp.where(equal, 1.0, 0.0).astype(BF16)


def column(row):
    return jnp.transpose(jnp.broadcast_to(row.astype(F32), (8, row.shape[1])))[:, 0:1].astype(jnp.int32)


def build_operators(coup, even_ops, odd_ops):
    wide = 384
    r = iota((BLOCK, wide), 0)
    c = iota((BLOCK, wide), 1)
    at = (
        (c >= BLOCK).astype(jnp.int32)
        + (c >= 2 * BLOCK).astype(jnp.int32)
        + (c >= 3 * BLOCK).astype(jnp.int32)
        + (c >= 4 * BLOCK).astype(jnp.int32)
    )
    jr = r & 7
    jc = c & 7
    same_j = jr == jc
    even_sum = ((jr + jc) & 1) == 0
    two_jc = (2 * jc + 1).astype(F32)
    d_j = jnp.where((jc < jr) & ~even_sum, two_jc, 0.0)
    delta_j = jnp.where(same_j, 1.0, 0.0)
    pair_j = jnp.where(even_sum, 2.0, 0.0)
    parity_jc = jnp.where((jc & 1) == 0, 1.0, -1.0)

    spread_f = jnp.where((iota((BLOCK, F), 0) >> 3) == iota((BLOCK, F), 1), 1.0, 0.0)
    cg = iota((F, wide), 1)
    cg_at = (
        (cg >= BLOCK).astype(jnp.int32)
        + (cg >= 2 * BLOCK).astype(jnp.int32)
        + (cg >= 3 * BLOCK).astype(jnp.int32)
        + (cg >= 4 * BLOCK).astype(jnp.int32)
    )
    spread_g = jnp.where(((cg - cg_at * BLOCK) >> 3) == iota((F, wide), 0), 1.0, 0.0)
    c0, c1, c2, c3 = (
        exact_dot(exact_dot(spread_f, coup[k], NT), spread_g) for k in range(4)
    )

    def build(ops, own, other, store):
        first = own[0]
        valid = at < len(own)
        ic = 2 * at + first
        two_ic = (2 * ic + 1).astype(F32)
        zero = jnp.zeros((BLOCK, wide), F32)
        blocks = [
            jnp.where(valid, c3 * delta_j, zero),
            jnp.where(valid & (ic == jr), c3 * parity_jc, zero),
            jnp.where(valid & (ic == jr), c3, zero),
        ]
        for i in other:
            if i > 0:
                blocks.append(jnp.where(valid & (ic < i), c0 * delta_j * two_ic, zero))
        for i in own:
            blocks.append(jnp.where(valid & (ic == i), c1 * d_j, zero))
        for i in own:
            same_i = ic == i
            here = c3 * (2.0 * delta_j + jnp.where(same_i, pair_j, 0.0))
            here = here + jnp.where(same_i, c2 * delta_j, 0.0)
            blocks.append(jnp.where(valid, here, zero))
        for at_row, block in enumerate(blocks):
            store(ops, at_row * BLOCK, block)

    def store_even(ops, row, block):
        high = block.astype(BF16).astype(F32)
        low = block - high
        rows = pl.ds(row, BLOCK)
        ops[rows, 0:256] = high[:, 0:256].astype(BF16)
        shared = high[:, 256:384] + pltpu.roll(low[:, 256:384], 64, 1)
        ops[rows, 256:384] = shared.astype(BF16)
        ops[rows, 384:640] = low[:, 0:256].astype(BF16)
        ops[rows, 640:896] = high[:, 0:256].astype(BF16)
        ops[rows, 896:1024] = high[:, 256:384].astype(BF16)

    def store_odd(ops, row, block):
        high, low = halves(block[:, 0:256])
        rows = pl.ds(row, BLOCK)
        ops[rows, 0:256] = high
        ops[rows, 256:512] = low
        ops[rows, 512:768] = high

    build(even_ops, EVEN, ODD, store_even)
    build(odd_ops, ODD, EVEN, store_odd)


def kernel(
    n,
    lam,
    order,
    send_index,
    recv_slot,
    grad,
    metric,
    step,
    coup,
    neighbour,
    neighbour_face,
    orient,
    halo_send,
    out_two,
    out_res,
    x_in,
    g_in,
    compact,
    send_buf,
    recv_buf,
    oh_slot,
    oh_local,
    oh_ghost,
    oh_halo,
    even_ops,
    odd_ops,
    even_v,
    odd_v,
    field,
    masks,
    traces,
    trace_halves,
    faces_send,
    faces_recv,
    halo_out,
    halo_in,
    even_res,
    odd_res,
    across,
    res_out,
    two_out,
    local_sem,
    move_send,
    move_recv,
    face_send_sem,
    face_recv_sem,
    halo_send_sem,
    halo_recv_sem,
):
    me = lax.axis_index("dev")
    cap = E // n
    chunk = 4 * cap
    above = lax.rem(me + 1, n)
    below = lax.rem(me + n - 1, n)
    barrier = pltpu.get_barrier_semaphore()

    x_copy = pltpu.make_async_copy(lam, x_in, local_sem.at[0])
    x_copy.start()
    g_copy = pltpu.make_async_copy(grad, g_in, local_sem.at[1])
    g_copy.start()

    def greet(j, carry):
        pl.semaphore_signal(barrier, inc=1, device_id=(lax.rem(me + j, n),), device_id_type=pl.DeviceIdType.MESH)
        return carry

    lax.fori_loop(1, n, greet, 0)

    oh_send = one_hot(column(send_index[...]) == iota((E, E), 1))
    tail = jnp.where(iota((E - F * M * M, E), 0) == 0, order[...].astype(F32), 0.0)
    compact[pl.ds(F * M * M, E - F * M * M), :] = tail
    x_copy.wait()
    for at, i in enumerate(PLACE):
        for f in range(F):
            compact[pl.ds(M * (at * F + f), M), :] = x_in[f, i]
    high, low = halves(compact[...])
    sorted_rows = dot(oh_send, high, NT) + dot(oh_send, low, NT)
    for part in range(4):
        send_buf[pl.ds(part, E, stride=4), :] = sorted_rows[:, 128 * part : 128 * (part + 1)]

    pl.semaphore_wait(barrier, n - 1)

    def piece(p):
        return pl.ds(pl.multiple_of(p * chunk, chunk), chunk)

    def move(j, carry):
        p = lax.rem(me + j, n)
        pltpu.make_async_remote_copy(
            src_ref=send_buf.at[piece(p), :],
            dst_ref=recv_buf.at[piece(me), :],
            send_sem=move_send,
            recv_sem=move_recv,
            device_id=(p,),
            device_id_type=pl.DeviceIdType.MESH,
        ).start()
        return carry

    lax.fori_loop(1, n, move, 0)
    own = pltpu.make_async_copy(send_buf.at[piece(me), :], recv_buf.at[piece(me), :], local_sem.at[2])
    own.start()

    rows = iota((E, E), 0)
    for k in range(4):
        name = neighbour[pl.ds(k, 1), :]
        oh_local[:, E * k : E * (k + 1)] = one_hot(rows == name)
        oh_ghost[:, E * k : E * (k + 1)] = one_hot(rows == name - E)
    for side in range(2):
        oh_halo[:, HALO * side : HALO * (side + 1)] = one_hot(
            iota((E, HALO), 0) == halo_send[pl.ds(side, 1), :]
        )

    wanted = jnp.zeros((16, E), F32)
    for k in range(4):
        face_row = jnp.broadcast_to(neighbour_face[pl.ds(k, 1), :].astype(F32), (16, E)).astype(BF16)
        wanted = wanted + dot(face_row, oh_ghost[:, E * k : E * (k + 1)], NT)
    faces_send[0] = wanted[0:8, 0:HALO]
    faces_send[1] = wanted[0:8, HALO:E]
    tell_below = pltpu.make_async_remote_copy(
        src_ref=faces_send.at[0],
        dst_ref=faces_recv.at[1],
        send_sem=face_send_sem.at[0],
        recv_sem=face_recv_sem.at[1],
        device_id=(below,),
        device_id_type=pl.DeviceIdType.MESH,
    )
    tell_above = pltpu.make_async_remote_copy(
        src_ref=faces_send.at[1],
        dst_ref=faces_recv.at[0],
        send_sem=face_send_sem.at[1],
        recv_sem=face_recv_sem.at[0],
        device_id=(above,),
        device_id_type=pl.DeviceIdType.MESH,
    )
    tell_below.start()
    tell_above.start()

    oh_slot[...] = one_hot(column(recv_slot[...]) == iota((E, E), 1))
    build_operators(coup, even_ops, odd_ops)
    even_v[pl.ds(960, 64), :] = jnp.zeros((64, E), BF16)
    for part in range(3):
        odd_v[pl.ds(256 * part + 240, 16), :] = jnp.zeros((16, E), BF16)
    g_copy.wait()
    tell_below.wait()
    tell_above.wait()

    own.wait()
    everyone = pl.ds(0, (n - 1) * chunk)
    arrived = pltpu.make_async_remote_copy(
        src_ref=send_buf.at[everyone, :],
        dst_ref=recv_buf.at[everyone, :],
        send_sem=move_send,
        recv_sem=move_recv,
        device_id=(above,),
        device_id_type=pl.DeviceIdType.MESH,
    )
    arrived.wait_recv()
    for part in range(4):
        flat = jnp.transpose(recv_buf[pl.ds(part, E, stride=4), :])
        high, low = halves(flat)
        compact[pl.ds(128 * part, 128), :] = dot(high, oh_slot[...]) + dot(low, oh_slot[...])

    order_row = compact[pl.ds(F * M * M, 1), :]
    lane_mode = iota((8, E), 0).astype(F32)
    mask_j = jnp.where(lane_mode <= order_row, 1.0, 0.0)
    for i in range(M):
        masks[i] = jnp.where(order_row >= float(i), mask_j, 0.0)

    def keep_halves(at, value):
        high, low = halves(value)
        if at < 3:
            even_v[pl.ds(BLOCK * at, BLOCK), :] = high
        else:
            even_v[pl.ds(240, 16), :] = high[0:16]
            even_v[pl.ds(256, 64), :] = high[16:80]
            even_v[pl.ds(320, 64), :] = high[16:80]
        if at < 3:
            even_v[pl.ds(384 + BLOCK * at, BLOCK), :] = high
        else:
            even_v[pl.ds(384 + 240, 16), :] = high[0:16]
        even_v[pl.ds(640 + BLOCK * at, BLOCK), :] = low

    def keep_odd_halves(at, value):
        high, low = halves(value)
        odd_v[pl.ds(BLOCK * at, BLOCK), :] = high
        odd_v[pl.ds(256 + BLOCK * at, BLOCK), :] = high
        odd_v[pl.ds(512 + BLOCK * at, BLOCK), :] = low

    def set_field(at, value):
        field[pl.ds(BLOCK * at, BLOCK), :] = value
        if at < 4:
            keep_halves(at, value)
        else:
            keep_odd_halves(at - 4, value)

    for at, i in enumerate(PLACE):
        mask = masks[i]
        parts = [compact[pl.ds(M * (at * F + f), 8), :] * mask for f in range(F)]
        set_field(at, jnp.concatenate(parts, axis=0))

    odd_row = (iota((8, E), 0) & 1) == 1
    m0 = metric[pl.ds(0, 1), :]
    m1 = metric[pl.ds(1, 1), :]
    pace = step[...]

    def send_halo(sweep):
        picked = dot(trace_halves[...], oh_halo[...])
        picked = picked[0:320] + picked[320:640]
        for side in range(2):
            face = faces_recv[side][0:1, :]
            lanes = slice(HALO * side, HALO * (side + 1))
            chosen = picked[240:320, lanes]
            for k in (2, 1, 0):
                chosen = jnp.where(face == float(k), picked[80 * k : 80 * (k + 1), lanes], chosen)
            halo_out[sweep, side] = chosen
        down = pltpu.make_async_remote_copy(
            src_ref=halo_out.at[sweep, 0],
            dst_ref=halo_in.at[sweep, 1],
            send_sem=halo_send_sem.at[sweep, 0],
            recv_sem=halo_recv_sem.at[sweep, 1],
            device_id=(below,),
            device_id_type=pl.DeviceIdType.MESH,
        )
        up = pltpu.make_async_remote_copy(
            src_ref=halo_out.at[sweep, 1],
            dst_ref=halo_in.at[sweep, 0],
            send_sem=halo_send_sem.at[sweep, 1],
            recv_sem=halo_recv_sem.at[sweep, 0],
            device_id=(above,),
            device_id_type=pl.DeviceIdType.MESH,
        )
        down.start()
        up.start()
        return down, up

    def residual(sweep, finish):
        from_even = dot(even_ops[pl.ds(0, 240), :], even_v[...])
        from_odd = dot(odd_ops[pl.ds(0, 240), :], odd_v[...])
        traces[0] = from_even[80:160] + from_odd[80:160]
        traces[1] = from_even[0:80] + from_odd[0:80]
        traces[2] = from_even[160:240] + from_odd[160:240]
        traces[3] = from_even[0:80] - from_odd[0:80]
        for k in range(4):
            high, low = halves(traces[k])
            trace_halves[pl.ds(80 * k, 80), :] = high
            trace_halves[pl.ds(320 + 80 * k, 80), :] = low
        down, up = send_halo(sweep)

        for k in range(4):
            got = dot(trace_halves[...], oh_local[:, E * k : E * (k + 1)])
            got = got[0:320] + got[320:640]
            face = neighbour_face[pl.ds(k, 1), :]
            chosen = got[240:320]
            for other in (2, 1, 0):
                chosen = jnp.where(face == other, got[80 * other : 80 * (other + 1)], chosen)
            across[k] = chosen
        even_res[...] = dot(even_ops[pl.ds(240, 880), :], even_v[...])
        odd_res[...] = dot(odd_ops[pl.ds(240, 720), :], odd_v[...])

        down.wait()
        up.wait()
        ghost = jnp.concatenate([halo_in[sweep, 0], halo_in[sweep, 1]], axis=1)
        ghost_halves = jnp.concatenate(list(halves(ghost)), axis=0)
        for k in range(4):
            got = dot(ghost_halves, oh_ghost[:, E * k : E * (k + 1)])
            turned = jnp.where(odd_row & (orient[pl.ds(k, 1), :] == 1), -1.0, 1.0)
            turned = jnp.concatenate([turned] * F, axis=0)
            across[k] = (across[k] + got[0:80] + got[80:160]) * turned
        south = across[0]
        north = across[2]
        across[0] = north + south
        across[2] = north - south
        east = across[1]
        west = across[3]
        across[1] = east + west
        across[3] = east - west

        for at, i in enumerate(PLACE):
            if i % 2 == 0:
                here = m1 * even_res[pl.ds(240 + BLOCK * at, BLOCK), :]
                here = here + even_res[pl.ds(560 + BLOCK * at, BLOCK), :]
                if i > 0:
                    here = here + m0 * odd_res[pl.ds(BLOCK * (at - 1), BLOCK), :]
                here = here - across[1]
            else:
                here = m1 * odd_res[pl.ds(240 + BLOCK * (at - 4), BLOCK), :]
                here = here + odd_res[pl.ds(480 + BLOCK * (at - 4), BLOCK), :]
                here = here + m0 * even_res[pl.ds(BLOCK * (at - 4), BLOCK), :]
                here = here - across[3]
            mask = masks[i]
            parts = []
            for f in range(F):
                plus = jnp.broadcast_to(across[0, pl.ds(8 * f + i, 1), :], (8, E))
                minus = jnp.broadcast_to(across[2, pl.ds(8 * f + i, 1), :], (8, E))
                lift = jnp.where(odd_row, minus, plus)
                goal = jnp.concatenate([g_in[f, i], jnp.zeros((1, E), F32)], axis=0)
                parts.append((here[8 * f : 8 * f + 8] - lift - goal) * mask)
            value = jnp.concatenate(parts, axis=0)
            finish(at, i, value, field[pl.ds(BLOCK * at, BLOCK), :] - pace * value)

    def next_field(at, i, value, advanced):
        set_field(at, advanced)

    def results(at, i, value, advanced):
        for f in range(F):
            res_out[f, i] = value[8 * f : 8 * f + M]
            two_out[f, i] = advanced[8 * f : 8 * f + M]

    residual(0, next_field)
    residual(1, results)
    copy_res = pltpu.make_async_copy(res_out, out_res, local_sem.at[3])
    copy_two = pltpu.make_async_copy(two_out, out_two, local_sem.at[4])
    copy_res.start()
    copy_two.start()
    arrived.wait_send()
    copy_res.wait()
    copy_two.wait()


def shards(n, *args):
    (lam, order, send_index, recv_slot, grad, metric, step, coup, neighbour, neighbour_face, orient, halo_send) = args
    in_vmem = pl.BlockSpec(memory_space=pltpu.VMEM)
    anywhere = pl.BlockSpec(memory_space=pl.ANY)
    shape = jax.ShapeDtypeStruct((F, M, M, E), F32)
    return pl.pallas_call(
        functools.partial(kernel, n),
        out_shape=(shape, shape),
        in_specs=[
            anywhere,
            in_vmem,
            in_vmem,
            in_vmem,
            anywhere,
            in_vmem,
            in_vmem,
            in_vmem,
            in_vmem,
            in_vmem,
            in_vmem,
            in_vmem,
        ],
        out_specs=(anywhere, anywhere),
        scratch_shapes=[
            pltpu.VMEM((F, M, M, E), F32),
            pltpu.VMEM((F, M, M, E), F32),
            pltpu.VMEM((E, E), F32),
            pltpu.VMEM((4 * E, 128), F32),
            pltpu.VMEM((4 * E, 128), F32),
            pltpu.VMEM((E, E), BF16),
            pltpu.VMEM((E, 4 * E), BF16),
            pltpu.VMEM((E, 4 * E), BF16),
            pltpu.VMEM((E, E), BF16),
            pltpu.VMEM((14 * BLOCK, 1024), BF16),
            pltpu.VMEM((12 * BLOCK, 768), BF16),
            pltpu.VMEM((1024, E), BF16),
            pltpu.VMEM((768, E), BF16),
            pltpu.VMEM((ROWS, E), F32),
            pltpu.VMEM((M, 8, E), F32),
            pltpu.VMEM((4, BLOCK, E), F32),
            pltpu.VMEM((8 * BLOCK, E), BF16),
            pltpu.VMEM((2, 8, HALO), F32),
            pltpu.VMEM((2, 8, HALO), F32),
            pltpu.VMEM((2, 2, BLOCK, HALO), F32),
            pltpu.VMEM((2, 2, BLOCK, HALO), F32),
            pltpu.VMEM((11 * BLOCK, E), F32),
            pltpu.VMEM((9 * BLOCK, E), F32),
            pltpu.VMEM((4, BLOCK, E), F32),
            pltpu.VMEM((F, M, M, E), F32),
            pltpu.VMEM((F, M, M, E), F32),
            pltpu.SemaphoreType.DMA((5,)),
            pltpu.SemaphoreType.DMA,
            pltpu.SemaphoreType.DMA,
            pltpu.SemaphoreType.DMA((2,)),
            pltpu.SemaphoreType.DMA((2,)),
            pltpu.SemaphoreType.DMA((2, 2)),
            pltpu.SemaphoreType.DMA((2, 2)),
        ],
        compiler_params=pltpu.CompilerParams(
            collective_id=0, has_side_effects=True, vmem_limit_bytes=48 * 1024 * 1024
        ),
    )(
        lam,
        order.reshape(1, E),
        send_index,
        recv_slot,
        grad,
        metric,
        step.reshape(1, E),
        coup,
        neighbour,
        neighbour_face,
        orient,
        halo_send,
    )


def solution(mesh):
    in_specs = (
        P(None, None, None, "dev"),
        P("dev"),
        P("dev", None),
        P("dev", None),
        P(None, None, None, "dev"),
        P(None, "dev"),
        P("dev"),
        P(),
        P(None, "dev"),
        P(None, "dev"),
        P(None, "dev"),
        P(None, "dev"),
    )
    out_specs = (P(None, None, None, "dev"), P(None, None, None, "dev"))
    return jax.shard_map(
        functools.partial(shards, mesh.shape["dev"]),
        mesh=mesh,
        in_specs=in_specs,
        out_specs=out_specs,
        check_vma=False,
    )
```

```python
import functools

import jax
import jax.numpy as jnp
from jax import lax
from jax.experimental import pallas as pl
from jax.experimental.pallas import tpu as pltpu
from jax.sharding import PartitionSpec as P

F = 10
M = 7
E = 512
HALO = 256
PLACE = (0, 2, 4, 6, 1, 3, 5)
EVEN = (0, 2, 4, 6)
ODD = (1, 3, 5)
BLOCK = 8 * F
ROWS = M * BLOCK
NN = (((1,), (0,)), ((), ()))
NT = (((1,), (1,)), ((), ()))
F32 = jnp.float32
BF16 = jnp.bfloat16


def send_order(sizes):
    left = [
        (a, b, c, d)
        for d in range(sizes[3])
        for c in range(sizes[2])
        for b in range(sizes[1])
        for a in range(sizes[0])
    ][1:]

    def hops(offset):
        load = []
        for step, size in zip(offset[:3], sizes):
            back = size - step if step else 0
            load += [step * (step <= back), back * (back <= step)]
            if step and step == back:
                load[-2:] = [step / 2, back / 2]
        return load

    total = [0.0] * 6
    order = []
    while left:

        def score(offset):
            load = [a + b for a, b in zip(total, hops(offset))]
            even = max(load) - min(load) + 0.01 * sum(v * v for v in load) / (1 + sum(load))
            return even - 0.3 * sum(hops(offset))

        best = min(left, key=score)
        left.remove(best)
        order.append(best)
        total = [a + b for a, b in zip(total, hops(best))]
    return order


def iota(shape, dim):
    return lax.broadcasted_iota(jnp.int32, shape, dim)


def dot(a, b, dims=NN):
    return lax.dot_general(a, b, dims, preferred_element_type=F32)


def exact_dot(a, b, dims=NN):
    return lax.dot_general(
        a, b, dims, precision=lax.Precision.HIGHEST, preferred_element_type=F32
    )


def halves(value):
    high = value.astype(BF16)
    low = (value - high.astype(F32)).astype(BF16)
    return high, low


def one_hot(equal):
    return jnp.where(equal, 1.0, 0.0).astype(BF16)


def column(row):
    return jnp.transpose(jnp.broadcast_to(row.astype(F32), (8, row.shape[1])))[:, 0:1].astype(jnp.int32)


def build_operators(coup, even_ops, odd_ops):
    wide = 384
    r = iota((BLOCK, wide), 0)
    c = iota((BLOCK, wide), 1)
    at = (
        (c >= BLOCK).astype(jnp.int32)
        + (c >= 2 * BLOCK).astype(jnp.int32)
        + (c >= 3 * BLOCK).astype(jnp.int32)
        + (c >= 4 * BLOCK).astype(jnp.int32)
    )
    jr = r & 7
    jc = c & 7
    same_j = jr == jc
    even_sum = ((jr + jc) & 1) == 0
    two_jc = (2 * jc + 1).astype(F32)
    d_j = jnp.where((jc < jr) & ~even_sum, two_jc, 0.0)
    delta_j = jnp.where(same_j, 1.0, 0.0)
    pair_j = jnp.where(even_sum, 2.0, 0.0)
    parity_jc = jnp.where((jc & 1) == 0, 1.0, -1.0)

    spread_f = jnp.where((iota((BLOCK, F), 0) >> 3) == iota((BLOCK, F), 1), 1.0, 0.0)
    cg = iota((F, wide), 1)
    cg_at = (
        (cg >= BLOCK).astype(jnp.int32)
        + (cg >= 2 * BLOCK).astype(jnp.int32)
        + (cg >= 3 * BLOCK).astype(jnp.int32)
        + (cg >= 4 * BLOCK).astype(jnp.int32)
    )
    spread_g = jnp.where(((cg - cg_at * BLOCK) >> 3) == iota((F, wide), 0), 1.0, 0.0)
    c0, c1, c2, c3 = (
        exact_dot(exact_dot(spread_f, coup[:, k, :], NT), spread_g) for k in range(4)
    )

    def build(ops, own, other, store):
        first = own[0]
        valid = at < len(own)
        ic = 2 * at + first
        two_ic = (2 * ic + 1).astype(F32)
        zero = jnp.zeros((BLOCK, wide), F32)
        blocks = [
            jnp.where(valid, c3 * delta_j, zero),
            jnp.where(valid & (ic == jr), c3 * parity_jc, zero),
            jnp.where(valid & (ic == jr), c3, zero),
        ]
        for i in other:
            if i > 0:
                blocks.append(jnp.where(valid & (ic < i), c0 * delta_j * two_ic, zero))
        for i in own:
            blocks.append(jnp.where(valid & (ic == i), c1 * d_j, zero))
        for i in own:
            same_i = ic == i
            here = c3 * (2.0 * delta_j + jnp.where(same_i, pair_j, 0.0))
            here = here + jnp.where(same_i, c2 * delta_j, 0.0)
            blocks.append(jnp.where(valid, here, zero))
        for at_row, block in enumerate(blocks):
            store(ops, at_row * BLOCK, block)

    def store_even(ops, row, block):
        high = block.astype(BF16).astype(F32)
        low = block - high
        rows = pl.ds(row, BLOCK)
        ops[rows, 0:256] = high[:, 0:256].astype(BF16)
        shared = high[:, 256:384] + pltpu.roll(low[:, 256:384], 64, 1)
        ops[rows, 256:384] = shared.astype(BF16)
        ops[rows, 384:640] = low[:, 0:256].astype(BF16)
        ops[rows, 640:896] = high[:, 0:256].astype(BF16)
        ops[rows, 896:1024] = high[:, 256:384].astype(BF16)

    def store_odd(ops, row, block):
        high, low = halves(block[:, 0:256])
        rows = pl.ds(row, BLOCK)
        ops[rows, 0:256] = high
        ops[rows, 256:512] = low
        ops[rows, 512:768] = high

    build(even_ops, EVEN, ODD, store_even)
    build(odd_ops, ODD, EVEN, store_odd)


def kernel(
    n,
    lam,
    order_far,
    send_far,
    recv_far,
    grad,
    metric_far,
    step_far,
    coup_far,
    neighbour_far,
    face_far,
    orient_far,
    halo_far,
    two_out,
    res_out,
    x_in,
    g_in,
    order,
    send_index,
    recv_slot,
    metric,
    step,
    coup,
    neighbour,
    neighbour_face,
    orient,
    halo_send,
    compact,
    send_buf,
    recv_buf,
    oh_slot,
    oh_local,
    oh_ghost,
    oh_halo,
    even_ops,
    odd_ops,
    even_v,
    odd_v,
    field,
    masks,
    traces,
    trace_halves,
    faces_send,
    faces_recv,
    halo_out,
    halo_in,
    even_res,
    odd_res,
    across,
    input_sem,
    local_sem,
    move_send,
    move_recv,
    face_send_sem,
    face_recv_sem,
    halo_send_sem,
    halo_recv_sem,
):
    me = lax.axis_index("dev")
    cap = E // n
    chunk = 4 * cap
    above = lax.rem(me + 1, n)
    below = lax.rem(me + n - 1, n)
    barrier = pltpu.get_barrier_semaphore()

    fetches = [
        pltpu.make_async_copy(far, near, input_sem.at[at])
        for at, (far, near) in enumerate(
            (
                (send_far, send_index),
                (order_far, order),
                (lam, x_in),
                (neighbour_far, neighbour),
                (face_far, neighbour_face),
                (halo_far, halo_send),
                (recv_far, recv_slot),
                (coup_far, coup),
                (orient_far, orient),
                (metric_far, metric),
                (step_far, step),
                (grad, g_in),
            )
        )
    ]
    for fetch in fetches:
        fetch.start()

    def greet(j, carry):
        pl.semaphore_signal(barrier, inc=1, device_id=(lax.rem(me + j, n),), device_id_type=pl.DeviceIdType.MESH)
        return carry

    lax.fori_loop(1, n, greet, 0)

    fetches[0].wait()
    fetches[1].wait()
    oh_send = one_hot(column(send_index[...]) == iota((E, E), 1))
    tail = jnp.where(iota((E - F * M * M, E), 0) == 0, order[...].astype(F32), 0.0)
    compact[pl.ds(F * M * M, E - F * M * M), :] = tail
    fetches[2].wait()
    for at, i in enumerate(PLACE):
        for f in range(F):
            compact[pl.ds(M * (at * F + f), M), :] = x_in[f, i]
    high, low = halves(compact[...])
    sorted_rows = dot(oh_send, high, NT) + dot(oh_send, low, NT)
    for part in range(4):
        send_buf[pl.ds(part, E, stride=4), :] = sorted_rows[:, 128 * part : 128 * (part + 1)]

    pl.semaphore_wait(barrier, n - 1)

    def piece(p):
        return pl.ds(pl.multiple_of(p * chunk, chunk), chunk)

    sizes = (n // 32, 4, 4, 2) if n >= 32 else (1, 1, n // 2, 2)
    core = lax.rem(me, 2)
    for offset in send_order(sizes):
        p = lax.rem(core + offset[3], 2)
        weight = 2
        place = me // 2
        for shift, size in zip(offset[2::-1], sizes[2::-1]):
            here = lax.rem(place, size)
            if shift:
                here = lax.rem(here + jnp.where(core == 0, shift, size - shift), size)
            p = p + weight * here
            weight = weight * size
            place = place // size
        pltpu.make_async_remote_copy(
            src_ref=send_buf.at[piece(p), :],
            dst_ref=recv_buf.at[piece(me), :],
            send_sem=move_send,
            recv_sem=move_recv,
            device_id=(p,),
            device_id_type=pl.DeviceIdType.MESH,
        ).start()
    own = pltpu.make_async_copy(send_buf.at[piece(me), :], recv_buf.at[piece(me), :], local_sem.at[0])
    own.start()

    for fetch in fetches[3:]:
        fetch.wait()
    rows = iota((E, E), 0)
    for k in range(4):
        name = neighbour[pl.ds(k, 1), :]
        oh_local[:, E * k : E * (k + 1)] = one_hot(rows == name)
        oh_ghost[:, E * k : E * (k + 1)] = one_hot(rows == name - E)
    for side in range(2):
        oh_halo[:, HALO * side : HALO * (side + 1)] = one_hot(
            iota((E, HALO), 0) == halo_send[pl.ds(side, 1), :]
        )

    wanted = jnp.zeros((16, E), F32)
    for k in range(4):
        face_row = jnp.broadcast_to(neighbour_face[pl.ds(k, 1), :].astype(F32), (16, E)).astype(BF16)
        wanted = wanted + dot(face_row, oh_ghost[:, E * k : E * (k + 1)], NT)
    faces_send[0] = wanted[0:8, 0:HALO]
    faces_send[1] = wanted[0:8, HALO:E]
    tell_below = pltpu.make_async_remote_copy(
        src_ref=faces_send.at[0],
        dst_ref=faces_recv.at[1],
        send_sem=face_send_sem.at[0],
        recv_sem=face_recv_sem.at[1],
        device_id=(below,),
        device_id_type=pl.DeviceIdType.MESH,
    )
    tell_above = pltpu.make_async_remote_copy(
        src_ref=faces_send.at[1],
        dst_ref=faces_recv.at[0],
        send_sem=face_send_sem.at[1],
        recv_sem=face_recv_sem.at[0],
        device_id=(above,),
        device_id_type=pl.DeviceIdType.MESH,
    )
    tell_below.start()
    tell_above.start()

    oh_slot[...] = one_hot(column(recv_slot[...]) == iota((E, E), 1))
    build_operators(coup, even_ops, odd_ops)
    even_v[pl.ds(960, 64), :] = jnp.zeros((64, E), BF16)
    for part in range(3):
        odd_v[pl.ds(256 * part + 240, 16), :] = jnp.zeros((16, E), BF16)
    tell_below.wait()
    tell_above.wait()

    own.wait()
    everyone = pl.ds(0, (n - 1) * chunk)
    arrived = pltpu.make_async_remote_copy(
        src_ref=send_buf.at[everyone, :],
        dst_ref=recv_buf.at[everyone, :],
        send_sem=move_send,
        recv_sem=move_recv,
        device_id=(above,),
        device_id_type=pl.DeviceIdType.MESH,
    )
    arrived.wait_recv()
    for part in range(4):
        flat = jnp.transpose(recv_buf[pl.ds(part, E, stride=4), :])
        high, low = halves(flat)
        compact[pl.ds(128 * part, 128), :] = dot(high, oh_slot[...]) + dot(low, oh_slot[...])

    order_row = compact[pl.ds(F * M * M, 1), :]
    lane_mode = iota((8, E), 0).astype(F32)
    mask_j = jnp.where(lane_mode <= order_row, 1.0, 0.0)
    for i in range(M):
        masks[i] = jnp.where(order_row >= float(i), mask_j, 0.0)

    def keep_halves(at, value):
        high, low = halves(value)
        if at < 3:
            even_v[pl.ds(BLOCK * at, BLOCK), :] = high
        else:
            even_v[pl.ds(240, 16), :] = high[0:16]
            even_v[pl.ds(256, 64), :] = high[16:80]
            even_v[pl.ds(320, 64), :] = high[16:80]
        if at < 3:
            even_v[pl.ds(384 + BLOCK * at, BLOCK), :] = high
        else:
            even_v[pl.ds(384 + 240, 16), :] = high[0:16]
        even_v[pl.ds(640 + BLOCK * at, BLOCK), :] = low

    def keep_odd_halves(at, value):
        high, low = halves(value)
        odd_v[pl.ds(BLOCK * at, BLOCK), :] = high
        odd_v[pl.ds(256 + BLOCK * at, BLOCK), :] = high
        odd_v[pl.ds(512 + BLOCK * at, BLOCK), :] = low

    def set_field(at, value):
        field[pl.ds(BLOCK * at, BLOCK), :] = value
        if at < 4:
            keep_halves(at, value)
        else:
            keep_odd_halves(at - 4, value)

    for at, i in enumerate(PLACE):
        mask = masks[i]
        parts = [compact[pl.ds(M * (at * F + f), 8), :] * mask for f in range(F)]
        set_field(at, jnp.concatenate(parts, axis=0))

    odd_row = (iota((8, E), 0) & 1) == 1
    m0 = metric[pl.ds(0, 1), :]
    m1 = metric[pl.ds(1, 1), :]
    pace = step[...]

    pending = []

    def send_halo(sweep):
        picked = dot(trace_halves[...], oh_halo[...])
        picked = picked[0:320] + picked[320:640]
        for side in range(2):
            face = faces_recv[side][0:1, :]
            lanes = slice(HALO * side, HALO * (side + 1))
            chosen = picked[240:320, lanes]
            for k in (2, 1, 0):
                chosen = jnp.where(face == float(k), picked[80 * k : 80 * (k + 1), lanes], chosen)
            halo_out[sweep, side] = chosen
        down = pltpu.make_async_remote_copy(
            src_ref=halo_out.at[sweep, 0],
            dst_ref=halo_in.at[sweep, 1],
            send_sem=halo_send_sem.at[sweep, 0],
            recv_sem=halo_recv_sem.at[sweep, 1],
            device_id=(below,),
            device_id_type=pl.DeviceIdType.MESH,
        )
        up = pltpu.make_async_remote_copy(
            src_ref=halo_out.at[sweep, 1],
            dst_ref=halo_in.at[sweep, 0],
            send_sem=halo_send_sem.at[sweep, 1],
            recv_sem=halo_recv_sem.at[sweep, 0],
            device_id=(above,),
            device_id_type=pl.DeviceIdType.MESH,
        )
        down.start()
        up.start()
        return down, up

    def residual(sweep, finish):
        from_even = dot(even_ops[pl.ds(0, 240), :], even_v[...])
        from_odd = dot(odd_ops[pl.ds(0, 240), :], odd_v[...])
        traces[0] = from_even[80:160] + from_odd[80:160]
        traces[1] = from_even[0:80] + from_odd[0:80]
        traces[2] = from_even[160:240] + from_odd[160:240]
        traces[3] = from_even[0:80] - from_odd[0:80]
        for k in range(4):
            high, low = halves(traces[k])
            trace_halves[pl.ds(80 * k, 80), :] = high
            trace_halves[pl.ds(320 + 80 * k, 80), :] = low
        down, up = send_halo(sweep)
        pending.extend((down, up))

        for k in range(4):
            got = dot(trace_halves[...], oh_local[:, E * k : E * (k + 1)])
            got = got[0:320] + got[320:640]
            face = neighbour_face[pl.ds(k, 1), :]
            chosen = got[240:320]
            for other in (2, 1, 0):
                chosen = jnp.where(face == other, got[80 * other : 80 * (other + 1)], chosen)
            across[k] = chosen
        even_res[...] = dot(even_ops[pl.ds(240, 880), :], even_v[...])
        odd_res[...] = dot(odd_ops[pl.ds(240, 720), :], odd_v[...])

        down.wait_recv()
        up.wait_recv()
        ghost = jnp.concatenate([halo_in[sweep, 0], halo_in[sweep, 1]], axis=1)
        ghost_halves = jnp.concatenate(list(halves(ghost)), axis=0)
        for k in range(4):
            got = dot(ghost_halves, oh_ghost[:, E * k : E * (k + 1)])
            turned = jnp.where(odd_row & (orient[pl.ds(k, 1), :] == 1), -1.0, 1.0)
            turned = jnp.concatenate([turned] * F, axis=0)
            across[k] = (across[k] + got[0:80] + got[80:160]) * turned
        south = across[0]
        north = across[2]
        across[0] = north + south
        across[2] = north - south
        east = across[1]
        west = across[3]
        across[1] = east + west
        across[3] = east - west

        for at, i in enumerate(PLACE):
            if i % 2 == 0:
                here = m1 * even_res[pl.ds(240 + BLOCK * at, BLOCK), :]
                here = here + even_res[pl.ds(560 + BLOCK * at, BLOCK), :]
                if i > 0:
                    here = here + m0 * odd_res[pl.ds(BLOCK * (at - 1), BLOCK), :]
                here = here - across[1]
            else:
                here = m1 * odd_res[pl.ds(240 + BLOCK * (at - 4), BLOCK), :]
                here = here + odd_res[pl.ds(480 + BLOCK * (at - 4), BLOCK), :]
                here = here + m0 * even_res[pl.ds(BLOCK * (at - 4), BLOCK), :]
                here = here - across[3]
            mask = masks[i]
            parts = []
            for f in range(F):
                plus = jnp.broadcast_to(across[0, pl.ds(8 * f + i, 1), :], (8, E))
                minus = jnp.broadcast_to(across[2, pl.ds(8 * f + i, 1), :], (8, E))
                lift = jnp.where(odd_row, minus, plus)
                goal = jnp.concatenate([g_in[f, i], jnp.zeros((1, E), F32)], axis=0)
                parts.append((here[8 * f : 8 * f + 8] - lift - goal) * mask)
            value = jnp.concatenate(parts, axis=0)
            finish(at, i, value, field[pl.ds(BLOCK * at, BLOCK), :] - pace * value)

    def next_field(at, i, value, advanced):
        set_field(at, advanced)

    def results(at, i, value, advanced):
        for f in range(F):
            res_out[f, i] = value[8 * f : 8 * f + M]
            two_out[f, i] = advanced[8 * f : 8 * f + M]

    residual(0, next_field)
    residual(1, results)
    arrived.wait_send()
    for copy in pending:
        copy.wait_send()


def hand_out(two, res, out_two, out_res, sem):
    copies = [
        pltpu.make_async_copy(two, out_two, sem.at[0]),
        pltpu.make_async_copy(res, out_res, sem.at[1]),
    ]
    for copy in copies:
        copy.start()
    for copy in copies:
        copy.wait()


def shards(n, *args):
    (lam, order, send_index, recv_slot, grad, metric, step, coup, neighbour, neighbour_face, orient, halo_send) = args
    anywhere = pl.BlockSpec(memory_space=pl.ANY)
    shape = jax.ShapeDtypeStruct((F, M, M, E), F32)
    two, res = pl.pallas_call(
        functools.partial(kernel, n),
        out_shape=(pltpu.VMEM((F, M, M, E), F32),) * 2,
        in_specs=[pl.BlockSpec(memory_space=pltpu.HBM)] * 12,
        out_specs=(pl.BlockSpec(memory_space=pltpu.VMEM),) * 2,
        scratch_shapes=[
            pltpu.VMEM((F, M, M, E), F32),
            pltpu.VMEM((F, M, M, E), F32),
            pltpu.VMEM((1, E), jnp.int32),
            pltpu.VMEM((1, E), jnp.int32),
            pltpu.VMEM((1, E), jnp.int32),
            pltpu.VMEM((2, E), F32),
            pltpu.VMEM((1, E), F32),
            pltpu.VMEM((F, 4, F), F32),
            pltpu.VMEM((4, E), jnp.int32),
            pltpu.VMEM((4, E), jnp.int32),
            pltpu.VMEM((4, E), jnp.int32),
            pltpu.VMEM((2, HALO), jnp.int32),
            pltpu.VMEM((E, E), F32),
            pltpu.VMEM((4 * E, 128), F32),
            pltpu.VMEM((4 * E, 128), F32),
            pltpu.VMEM((E, E), BF16),
            pltpu.VMEM((E, 4 * E), BF16),
            pltpu.VMEM((E, 4 * E), BF16),
            pltpu.VMEM((E, E), BF16),
            pltpu.VMEM((14 * BLOCK, 1024), BF16),
            pltpu.VMEM((12 * BLOCK, 768), BF16),
            pltpu.VMEM((1024, E), BF16),
            pltpu.VMEM((768, E), BF16),
            pltpu.VMEM((ROWS, E), F32),
            pltpu.VMEM((M, 8, E), F32),
            pltpu.VMEM((4, BLOCK, E), F32),
            pltpu.VMEM((8 * BLOCK, E), BF16),
            pltpu.VMEM((2, 8, HALO), F32),
            pltpu.VMEM((2, 8, HALO), F32),
            pltpu.VMEM((2, 2, BLOCK, HALO), F32),
            pltpu.VMEM((2, 2, BLOCK, HALO), F32),
            pltpu.VMEM((11 * BLOCK, E), F32),
            pltpu.VMEM((9 * BLOCK, E), F32),
            pltpu.VMEM((4, BLOCK, E), F32),
            pltpu.SemaphoreType.DMA((12,)),
            pltpu.SemaphoreType.DMA((1,)),
            pltpu.SemaphoreType.DMA,
            pltpu.SemaphoreType.DMA,
            pltpu.SemaphoreType.DMA((2,)),
            pltpu.SemaphoreType.DMA((2,)),
            pltpu.SemaphoreType.DMA((2, 2)),
            pltpu.SemaphoreType.DMA((2, 2)),
        ],
        compiler_params=pltpu.CompilerParams(
            collective_id=0, has_side_effects=True, vmem_limit_bytes=60928 * 1024
        ),
    )(
        lam,
        order.reshape(1, E),
        send_index,
        recv_slot,
        grad,
        metric,
        step.reshape(1, E),
        jnp.transpose(coup, (1, 0, 2)),
        neighbour,
        neighbour_face,
        orient,
        halo_send,
    )
    return pl.pallas_call(
        hand_out,
        out_shape=(shape, shape),
        in_specs=[anywhere] * 2,
        out_specs=(anywhere, anywhere),
        scratch_shapes=[pltpu.SemaphoreType.DMA((2,))],
        compiler_params=pltpu.CompilerParams(vmem_limit_bytes=1024 * 1024),
    )(two, res)


def solution(mesh):
    in_specs = (
        P(None, None, None, "dev"),
        P("dev"),
        P("dev", None),
        P("dev", None),
        P(None, None, None, "dev"),
        P(None, "dev"),
        P("dev"),
        P(),
        P(None, "dev"),
        P(None, "dev"),
        P(None, "dev"),
        P(None, "dev"),
    )
    out_specs = (P(None, None, None, "dev"), P(None, None, None, "dev"))
    return jax.shard_map(
        functools.partial(shards, mesh.shape["dev"]),
        mesh=mesh,
        in_specs=in_specs,
        out_specs=out_specs,
        check_vma=False,
    )
```

```python
import functools

import jax
import jax.numpy as jnp
from jax import lax
from jax.experimental import pallas as pl
from jax.experimental.pallas import tpu as pltpu
from jax.sharding import PartitionSpec as P

F = 10
M = 7
E = 512
HALO = 256
PLACE = (0, 2, 4, 6, 1, 3, 5)
EVEN = (0, 2, 4, 6)
ODD = (1, 3, 5)
BLOCK = 8 * F
ROWS = M * BLOCK
NN = (((1,), (0,)), ((), ()))
NT = (((1,), (1,)), ((), ()))
F32 = jnp.float32
BF16 = jnp.bfloat16


def send_order(sizes):
    left = [
        (a, b, c, d)
        for d in range(sizes[3])
        for c in range(sizes[2])
        for b in range(sizes[1])
        for a in range(sizes[0])
    ][1:]

    def hops(offset):
        load = []
        for step, size in zip(offset[:3], sizes):
            back = size - step if step else 0
            load += [step * (step <= back), back * (back <= step)]
            if step and step == back:
                load[-2:] = [step / 2, back / 2]
        return load

    total = [0.0] * 6
    order = []
    while left:

        def score(offset):
            load = [a + b for a, b in zip(total, hops(offset))]
            even = max(load) - min(load) + 0.01 * sum(v * v for v in load) / (1 + sum(load))
            return even - 0.3 * sum(hops(offset))

        best = min(left, key=score)
        left.remove(best)
        order.append(best)
        total = [a + b for a, b in zip(total, hops(best))]
    return order


def iota(shape, dim):
    return lax.broadcasted_iota(jnp.int32, shape, dim)


def dot(a, b, dims=NN):
    return lax.dot_general(a, b, dims, preferred_element_type=F32)


def exact_dot(a, b, dims=NN):
    return lax.dot_general(
        a, b, dims, precision=lax.Precision.HIGHEST, preferred_element_type=F32
    )


def halves(value):
    high = value.astype(BF16)
    low = (value - high.astype(F32)).astype(BF16)
    return high, low


def one_hot(equal):
    return jnp.where(equal, 1.0, 0.0).astype(BF16)


def column(row):
    return jnp.transpose(jnp.broadcast_to(row.astype(F32), (8, row.shape[1])))[:, 0:1].astype(jnp.int32)


def build_operators(coup, even_ops, odd_ops):
    wide = 384
    r = iota((BLOCK, wide), 0)
    c = iota((BLOCK, wide), 1)
    at = (
        (c >= BLOCK).astype(jnp.int32)
        + (c >= 2 * BLOCK).astype(jnp.int32)
        + (c >= 3 * BLOCK).astype(jnp.int32)
        + (c >= 4 * BLOCK).astype(jnp.int32)
    )
    jr = r & 7
    jc = c & 7
    same_j = jr == jc
    even_sum = ((jr + jc) & 1) == 0
    two_jc = (2 * jc + 1).astype(F32)
    d_j = jnp.where((jc < jr) & ~even_sum, two_jc, 0.0)
    delta_j = jnp.where(same_j, 1.0, 0.0)
    pair_j = jnp.where(even_sum, 2.0, 0.0)
    parity_jc = jnp.where((jc & 1) == 0, 1.0, -1.0)

    spread_f = jnp.where((iota((BLOCK, F), 0) >> 3) == iota((BLOCK, F), 1), 1.0, 0.0)
    cg = iota((F, wide), 1)
    cg_at = (
        (cg >= BLOCK).astype(jnp.int32)
        + (cg >= 2 * BLOCK).astype(jnp.int32)
        + (cg >= 3 * BLOCK).astype(jnp.int32)
        + (cg >= 4 * BLOCK).astype(jnp.int32)
    )
    spread_g = jnp.where(((cg - cg_at * BLOCK) >> 3) == iota((F, wide), 0), 1.0, 0.0)
    c0, c1, c2, c3 = (
        exact_dot(exact_dot(spread_f, coup[:, k, :], NT), spread_g) for k in range(4)
    )

    def build(ops, own, other, store):
        first = own[0]
        valid = at < len(own)
        ic = 2 * at + first
        two_ic = (2 * ic + 1).astype(F32)
        zero = jnp.zeros((BLOCK, wide), F32)
        blocks = [
            jnp.where(valid, c3 * delta_j, zero),
            jnp.where(valid & (ic == jr), c3 * parity_jc, zero),
            jnp.where(valid & (ic == jr), c3, zero),
        ]
        for i in other:
            if i > 0:
                blocks.append(jnp.where(valid & (ic < i), c0 * delta_j * two_ic, zero))
        for i in own:
            blocks.append(jnp.where(valid & (ic == i), c1 * d_j, zero))
        for i in own:
            same_i = ic == i
            here = c3 * (2.0 * delta_j + jnp.where(same_i, pair_j, 0.0))
            here = here + jnp.where(same_i, c2 * delta_j, 0.0)
            blocks.append(jnp.where(valid, here, zero))
        for at_row, block in enumerate(blocks):
            store(ops, at_row * BLOCK, block)

    def store_even(ops, row, block):
        high = block.astype(BF16).astype(F32)
        low = block - high
        rows = pl.ds(row, BLOCK)
        ops[rows, 0:256] = high[:, 0:256].astype(BF16)
        shared = high[:, 256:384] + pltpu.roll(low[:, 256:384], 64, 1)
        ops[rows, 256:384] = shared.astype(BF16)
        ops[rows, 384:640] = low[:, 0:256].astype(BF16)
        ops[rows, 640:896] = high[:, 0:256].astype(BF16)
        ops[rows, 896:1024] = high[:, 256:384].astype(BF16)

    def store_odd(ops, row, block):
        high, low = halves(block[:, 0:256])
        rows = pl.ds(row, BLOCK)
        ops[rows, 0:256] = high
        ops[rows, 256:512] = low
        ops[rows, 512:768] = high

    build(even_ops, EVEN, ODD, store_even)
    build(odd_ops, ODD, EVEN, store_odd)


def residual_block(at, i, base, across, masks):
    odd_row = (iota((8, E), 0) & 1) == 1
    mask = masks[i]
    parts = []
    for f in range(F):
        plus = jnp.broadcast_to(across[0, pl.ds(8 * f + i, 1), :], (8, E))
        minus = jnp.broadcast_to(across[2, pl.ds(8 * f + i, 1), :], (8, E))
        lift = jnp.where(odd_row, minus, plus) + across[1 if i % 2 == 0 else 3, pl.ds(8 * f, 8), :]
        parts.append((base[pl.ds(BLOCK * at + 8 * f, 8), :] - lift) * mask)
    return jnp.concatenate(parts, axis=0)


def kernel(
    n,
    lam,
    order_far,
    send_far,
    recv_far,
    grad,
    metric_far,
    step_far,
    coup_far,
    neighbour_far,
    face_far,
    orient_far,
    halo_far,
    field,
    base,
    across,
    masks,
    pace_out,
    x_in,
    g_in,
    order,
    send_index,
    recv_slot,
    metric,
    step,
    coup,
    neighbour,
    neighbour_face,
    orient,
    halo_send,
    compact,
    send_buf,
    recv_buf,
    oh_slot,
    oh_local,
    oh_ghost,
    oh_halo,
    oh_halo_arrived,
    oh_local_arrived,
    even_ops,
    odd_ops,
    even_v,
    odd_v,
    traces,
    trace_halves,
    faces_send,
    faces_recv,
    halo_out,
    halo_in,
    even_res,
    odd_res,
    input_sem,
    local_sem,
    move_send,
    move_recv,
    face_send_sem,
    face_recv_sem,
    halo_send_sem,
    halo_recv_sem,
):
    me = lax.axis_index("dev")
    cap = E // n
    chunk = 4 * cap
    above = lax.rem(me + 1, n)
    below = lax.rem(me + n - 1, n)
    barrier = pltpu.get_barrier_semaphore()

    fetches = [
        pltpu.make_async_copy(far, near, input_sem.at[at])
        for at, (far, near) in enumerate(
            (
                (send_far, send_index),
                (order_far, order),
                (lam, x_in),
                (neighbour_far, neighbour),
                (face_far, neighbour_face),
                (halo_far, halo_send),
                (recv_far, recv_slot),
                (coup_far, coup),
                (orient_far, orient),
                (metric_far, metric),
                (step_far, step),
                (grad, g_in),
            )
        )
    ]
    for fetch in fetches:
        fetch.start()

    sizes = (n // 32, 4, 4, 2) if n >= 32 else (1, 1, n // 2, 2)
    core = lax.rem(me, 2)
    partners = []
    for offset in send_order(sizes):
        p = lax.rem(core + offset[3], 2)
        weight = 2
        place = me // 2
        for shift, size in zip(offset[2::-1], sizes[2::-1]):
            here = lax.rem(place, size)
            if shift:
                here = lax.rem(here + jnp.where(core == 0, shift, size - shift), size)
            p = p + weight * here
            weight = weight * size
            place = place // size
        partners.append(p)
    for p in partners:
        pl.semaphore_signal(barrier, inc=1, device_id=(p,), device_id_type=pl.DeviceIdType.MESH)

    fetches[0].wait()
    fetches[1].wait()
    oh_send = one_hot(column(send_index[...]) == iota((E, E), 1))
    tail = jnp.where(iota((E - F * M * M, E), 0) == 0, order[...].astype(F32), 0.0)
    compact[pl.ds(F * M * M, E - F * M * M), :] = tail
    fetches[2].wait()
    for at, i in enumerate(PLACE):
        for f in range(F):
            compact[pl.ds(M * (at * F + f), M), :] = x_in[f, i]
    high, low = halves(compact[...])
    sorted_rows = dot(oh_send, high, NT) + dot(oh_send, low, NT)
    for part in range(4):
        send_buf[pl.ds(part, E, stride=4), :] = sorted_rows[:, 128 * part : 128 * (part + 1)]

    for fetch in fetches[3:5]:
        fetch.wait()
    rows = iota((E, E), 0)
    for k in range(4):
        oh_ghost[:, E * k : E * (k + 1)] = one_hot(rows == neighbour[pl.ds(k, 1), :] - E)
    wanted = jnp.zeros((16, E), F32)
    for k in range(4):
        face_row = jnp.broadcast_to(neighbour_face[pl.ds(k, 1), :].astype(F32), (16, E)).astype(BF16)
        wanted = wanted + dot(face_row, oh_ghost[:, E * k : E * (k + 1)], NT)
    faces_send[0] = wanted[0:8, 0:HALO]
    faces_send[1] = wanted[0:8, HALO:E]
    tell_below = pltpu.make_async_remote_copy(
        src_ref=faces_send.at[0],
        dst_ref=faces_recv.at[1],
        send_sem=face_send_sem.at[0],
        recv_sem=face_recv_sem.at[1],
        device_id=(below,),
        device_id_type=pl.DeviceIdType.MESH,
    )
    tell_above = pltpu.make_async_remote_copy(
        src_ref=faces_send.at[1],
        dst_ref=faces_recv.at[0],
        send_sem=face_send_sem.at[1],
        recv_sem=face_recv_sem.at[0],
        device_id=(above,),
        device_id_type=pl.DeviceIdType.MESH,
    )
    pl.semaphore_wait(barrier, n - 1)
    tell_below.start()
    tell_above.start()

    def piece(p):
        return pl.ds(pl.multiple_of(p * chunk, chunk), chunk)

    def send(p):
        pltpu.make_async_remote_copy(
            src_ref=send_buf.at[piece(p), :],
            dst_ref=recv_buf.at[piece(me), :],
            send_sem=move_send,
            recv_sem=move_recv,
            device_id=(p,),
            device_id_type=pl.DeviceIdType.MESH,
        ).start()

    for p in partners:
        send(p)
    own = pltpu.make_async_copy(send_buf.at[piece(me), :], recv_buf.at[piece(me), :], local_sem.at[0])
    own.start()

    for fetch in fetches[5:]:
        fetch.wait()
    for k in range(4):
        name = neighbour[pl.ds(k, 1), :]
        oh_local[:, E * k : E * (k + 1)] = one_hot(rows == name)
    for side in range(2):
        oh_halo[:, HALO * side : HALO * (side + 1)] = one_hot(
            iota((E, HALO), 0) == halo_send[pl.ds(side, 1), :]
        )

    oh_slot[...] = one_hot(column(recv_slot[...]) == iota((E, E), 1))
    oh_halo_arrived[...] = dot(oh_slot[...], oh_halo[...]).astype(BF16)
    for k in range(4):
        lanes = slice(E * k, E * (k + 1))
        oh_local_arrived[:, lanes] = dot(oh_slot[...], oh_local[:, lanes]).astype(BF16)
    build_operators(coup, even_ops, odd_ops)
    even_v[pl.ds(960, 64), :] = jnp.zeros((64, E), BF16)
    base[...] = jnp.zeros((ROWS, E), F32)
    for part in range(3):
        odd_v[pl.ds(256 * part + 240, 16), :] = jnp.zeros((16, E), BF16)
    tell_below.wait()
    tell_above.wait()

    own.wait()
    everyone = pl.ds(0, (n - 1) * chunk)
    arrived = pltpu.make_async_remote_copy(
        src_ref=send_buf.at[everyone, :],
        dst_ref=recv_buf.at[everyone, :],
        send_sem=move_send,
        recv_sem=move_recv,
        device_id=(above,),
        device_id_type=pl.DeviceIdType.MESH,
    )
    arrived.wait_recv()
    for part in range(4):
        compact[pl.ds(128 * part, 128), :] = jnp.transpose(recv_buf[pl.ds(part, E, stride=4), :])

    mode_j = iota((8, E), 0).astype(F32)

    def mode_masks(order_row):
        mask_j = jnp.where(mode_j <= order_row, 1.0, 0.0)
        return [jnp.where(order_row >= float(i), mask_j, 0.0) for i in range(M)]

    order_arrived = compact[pl.ds(F * M * M, 1), :]

    def keep_halves(at, value):
        high, low = halves(value)
        if at < 3:
            even_v[pl.ds(BLOCK * at, BLOCK), :] = high
        else:
            even_v[pl.ds(240, 16), :] = high[0:16]
            even_v[pl.ds(256, 64), :] = high[16:80]
            even_v[pl.ds(320, 64), :] = high[16:80]
        if at < 3:
            even_v[pl.ds(384 + BLOCK * at, BLOCK), :] = high
        else:
            even_v[pl.ds(384 + 240, 16), :] = high[0:16]
        even_v[pl.ds(640 + BLOCK * at, BLOCK), :] = low

    def keep_odd_halves(at, value):
        high, low = halves(value)
        odd_v[pl.ds(BLOCK * at, BLOCK), :] = high
        odd_v[pl.ds(256 + BLOCK * at, BLOCK), :] = high
        odd_v[pl.ds(512 + BLOCK * at, BLOCK), :] = low

    def place_block(at, value):
        if at < 4:
            keep_halves(at, value)
        else:
            keep_odd_halves(at - 4, value)

    masks_arrived = mode_masks(order_arrived)
    for at, i in enumerate(PLACE):
        parts = [compact[pl.ds(M * (at * F + f), 8), :] * masks_arrived[i] for f in range(F)]
        place_block(at, jnp.concatenate(parts, axis=0))

    def set_field(at, value):
        field[pl.ds(BLOCK * at, BLOCK), :] = value
        place_block(at, value)

    def take_slots():
        order_rows = jnp.broadcast_to(order_arrived, (16, E)).astype(BF16)
        order_row = dot(order_rows, oh_slot[...])[0:1]
        for i, mask in enumerate(mode_masks(order_row)):
            masks[i] = mask
        high = jnp.concatenate([even_v[pl.ds(0, 320), :], odd_v[pl.ds(0, 240), :]], axis=0)
        low = jnp.concatenate([even_v[pl.ds(640, 320), :], odd_v[pl.ds(512, 240), :]], axis=0)
        high = dot(high, oh_slot[...])
        low = dot(low, oh_slot[...])
        field[...] = high + low
        high = high.astype(BF16)
        low = low.astype(BF16)
        even_v[pl.ds(0, 320), :] = high[0:320]
        even_v[pl.ds(320, 64), :] = high[256:320]
        even_v[pl.ds(384, 256), :] = high[0:256]
        even_v[pl.ds(640, 320), :] = low[0:320]
        odd_v[pl.ds(0, 240), :] = high[320:560]
        odd_v[pl.ds(256, 240), :] = high[320:560]
        odd_v[pl.ds(512, 240), :] = low[320:560]

    odd_row = (iota((8, E), 0) & 1) == 1
    m0 = metric[pl.ds(0, 1), :]
    m1 = metric[pl.ds(1, 1), :]
    pace = step[...]

    pending = []

    def send_halo(sweep, chosen_halo):
        picked = dot(trace_halves[...], chosen_halo[...])
        picked = picked[0:320] + picked[320:640]
        for side in range(2):
            face = faces_recv[side][0:1, :]
            lanes = slice(HALO * side, HALO * (side + 1))
            chosen = picked[240:320, lanes]
            for k in (2, 1, 0):
                chosen = jnp.where(face == float(k), picked[80 * k : 80 * (k + 1), lanes], chosen)
            halo_out[sweep, side] = chosen
        down = pltpu.make_async_remote_copy(
            src_ref=halo_out.at[sweep, 0],
            dst_ref=halo_in.at[sweep, 1],
            send_sem=halo_send_sem.at[sweep, 0],
            recv_sem=halo_recv_sem.at[sweep, 1],
            device_id=(below,),
            device_id_type=pl.DeviceIdType.MESH,
        )
        up = pltpu.make_async_remote_copy(
            src_ref=halo_out.at[sweep, 1],
            dst_ref=halo_in.at[sweep, 0],
            send_sem=halo_send_sem.at[sweep, 1],
            recv_sem=halo_recv_sem.at[sweep, 0],
            device_id=(above,),
            device_id_type=pl.DeviceIdType.MESH,
        )
        down.start()
        up.start()
        return down, up

    def turned(k):
        sign = jnp.where(odd_row & (orient[pl.ds(k, 1), :] == 1), -1.0, 1.0)
        return jnp.concatenate([sign] * F, axis=0)

    def combine(across):
        south = across[0]
        north = across[2]
        across[0] = north + south
        across[2] = north - south
        east = across[1]
        west = across[3]
        across[1] = east + west
        across[3] = east - west

    def residual(sweep, chosen_halo, chosen_local, before_volume, finish):
        from_even = dot(even_ops[pl.ds(0, 240), :], even_v[...])
        from_odd = dot(odd_ops[pl.ds(0, 240), :], odd_v[...])
        traces[0] = from_even[80:160] + from_odd[80:160]
        traces[1] = from_even[0:80] + from_odd[0:80]
        traces[2] = from_even[160:240] + from_odd[160:240]
        traces[3] = from_even[0:80] - from_odd[0:80]
        for k in range(4):
            high, low = halves(traces[k])
            trace_halves[pl.ds(80 * k, 80), :] = high
            trace_halves[pl.ds(320 + 80 * k, 80), :] = low
        down, up = send_halo(sweep, chosen_halo)
        pending.extend((down, up))

        for k in range(4):
            got = dot(trace_halves[...], chosen_local[:, E * k : E * (k + 1)])
            got = got[0:320] + got[320:640]
            face = neighbour_face[pl.ds(k, 1), :]
            chosen = got[240:320]
            for other in (2, 1, 0):
                chosen = jnp.where(face == other, got[80 * other : 80 * (other + 1)], chosen)
            across[k] = chosen * turned(k)
        combine(across)
        before_volume()
        even_res[...] = dot(even_ops[pl.ds(240, 880), :], even_v[...])
        odd_res[...] = dot(odd_ops[pl.ds(240, 720), :], odd_v[...])

        for at, i in enumerate(PLACE):
            if i % 2 == 0:
                here = m1 * even_res[pl.ds(240 + BLOCK * at, BLOCK), :]
                here = here + even_res[pl.ds(560 + BLOCK * at, BLOCK), :]
                if i > 0:
                    here = here + m0 * odd_res[pl.ds(BLOCK * (at - 1), BLOCK), :]
            else:
                here = m1 * odd_res[pl.ds(240 + BLOCK * (at - 4), BLOCK), :]
                here = here + odd_res[pl.ds(480 + BLOCK * (at - 4), BLOCK), :]
                here = here + m0 * even_res[pl.ds(BLOCK * (at - 4), BLOCK), :]
            for f in range(F):
                base[pl.ds(BLOCK * at + 8 * f, M), :] = here[8 * f : 8 * f + M] - g_in[f, i]

        down.wait_recv()
        up.wait_recv()
        ghost = jnp.concatenate([halo_in[sweep, 0], halo_in[sweep, 1]], axis=1)
        ghost_halves = jnp.concatenate(list(halves(ghost)), axis=0)
        beyond = []
        for k in range(4):
            got = dot(ghost_halves, oh_ghost[:, E * k : E * (k + 1)])
            beyond.append((got[0:80] + got[80:160]) * turned(k))
        across[0] = across[0] + (beyond[2] + beyond[0])
        across[2] = across[2] + (beyond[2] - beyond[0])
        across[1] = across[1] + (beyond[1] + beyond[3])
        across[3] = across[3] + (beyond[1] - beyond[3])

        finish()

    def next_field():
        for at, i in enumerate(PLACE):
            value = residual_block(at, i, base, across, masks)
            set_field(at, field[pl.ds(BLOCK * at, BLOCK), :] - pace * value)

    residual(0, oh_halo_arrived, oh_local_arrived, take_slots, next_field)
    residual(1, oh_halo, oh_local, lambda: None, lambda: None)
    pace_out[...] = pace
    arrived.wait_send()
    for copy in pending:
        copy.wait_send()


def last_step(field, base, across, masks, pace, out_two, out_res, two, res, sem):
    copies = []
    for at, i in enumerate(PLACE):
        value = residual_block(at, i, base, across, masks)
        advanced = field[pl.ds(BLOCK * at, BLOCK), :] - pace[...] * value
        for f in range(F):
            res[f, i] = value[8 * f : 8 * f + M]
            two[f, i] = advanced[8 * f : 8 * f + M]
        for kind, (near, far) in enumerate(((two, out_two), (res, out_res))):
            copies.append(pltpu.make_async_copy(near.at[:, i], far.at[:, i], sem.at[kind, i]))
            copies[-1].start()
    for copy in copies:
        copy.wait()


def shards(n, *args):
    (lam, order, send_index, recv_slot, grad, metric, step, coup, neighbour, neighbour_face, orient, halo_send) = args
    anywhere = pl.BlockSpec(memory_space=pl.ANY)
    shape = jax.ShapeDtypeStruct((F, M, M, E), F32)
    kept = pl.pallas_call(
        functools.partial(kernel, n),
        out_shape=(
            pltpu.VMEM((ROWS, E), F32),
            pltpu.VMEM((ROWS, E), F32),
            pltpu.VMEM((4, BLOCK, E), F32),
            pltpu.VMEM((M, 8, E), F32),
            pltpu.VMEM((1, E), F32),
        ),
        in_specs=[pl.BlockSpec(memory_space=pltpu.HBM)] * 12,
        out_specs=(pl.BlockSpec(memory_space=pltpu.VMEM),) * 5,
        scratch_shapes=[
            pltpu.VMEM((F, M, M, E), F32),
            pltpu.VMEM((F, M, M, E), F32),
            pltpu.VMEM((1, E), jnp.int32),
            pltpu.VMEM((1, E), jnp.int32),
            pltpu.VMEM((1, E), jnp.int32),
            pltpu.VMEM((2, E), F32),
            pltpu.VMEM((1, E), F32),
            pltpu.VMEM((F, 4, F), F32),
            pltpu.VMEM((4, E), jnp.int32),
            pltpu.VMEM((4, E), jnp.int32),
            pltpu.VMEM((4, E), jnp.int32),
            pltpu.VMEM((2, HALO), jnp.int32),
            pltpu.VMEM((E, E), F32),
            pltpu.VMEM((4 * E, 128), F32),
            pltpu.VMEM((4 * E, 128), F32),
            pltpu.VMEM((E, E), BF16),
            pltpu.VMEM((E, 4 * E), BF16),
            pltpu.VMEM((E, 4 * E), BF16),
            pltpu.VMEM((E, E), BF16),
            pltpu.VMEM((E, E), BF16),
            pltpu.VMEM((E, 4 * E), BF16),
            pltpu.VMEM((14 * BLOCK, 1024), BF16),
            pltpu.VMEM((12 * BLOCK, 768), BF16),
            pltpu.VMEM((1024, E), BF16),
            pltpu.VMEM((768, E), BF16),
            pltpu.VMEM((4, BLOCK, E), F32),
            pltpu.VMEM((8 * BLOCK, E), BF16),
            pltpu.VMEM((2, 8, HALO), F32),
            pltpu.VMEM((2, 8, HALO), F32),
            pltpu.VMEM((2, 2, BLOCK, HALO), F32),
            pltpu.VMEM((2, 2, BLOCK, HALO), F32),
            pltpu.VMEM((11 * BLOCK, E), F32),
            pltpu.VMEM((9 * BLOCK, E), F32),
            pltpu.SemaphoreType.DMA((12,)),
            pltpu.SemaphoreType.DMA((1,)),
            pltpu.SemaphoreType.DMA,
            pltpu.SemaphoreType.DMA,
            pltpu.SemaphoreType.DMA((2,)),
            pltpu.SemaphoreType.DMA((2,)),
            pltpu.SemaphoreType.DMA((2, 2)),
            pltpu.SemaphoreType.DMA((2, 2)),
        ],
        compiler_params=pltpu.CompilerParams(
            collective_id=0, has_side_effects=True, vmem_limit_bytes=60928 * 1024
        ),
    )(
        lam,
        order.reshape(1, E),
        send_index,
        recv_slot,
        grad,
        metric,
        step.reshape(1, E),
        jnp.transpose(coup, (1, 0, 2)),
        neighbour,
        neighbour_face,
        orient,
        halo_send,
    )
    return pl.pallas_call(
        last_step,
        out_shape=(shape, shape),
        in_specs=[pl.BlockSpec(memory_space=pltpu.VMEM)] * 5,
        out_specs=(anywhere, anywhere),
        scratch_shapes=[
            pltpu.VMEM((F, M, M, E), F32),
            pltpu.VMEM((F, M, M, E), F32),
            pltpu.SemaphoreType.DMA((2, M)),
        ],
        compiler_params=pltpu.CompilerParams(vmem_limit_bytes=4 * 1024 * 1024),
    )(*kept)


def solution(mesh):
    in_specs = (
        P(None, None, None, "dev"),
        P("dev"),
        P("dev", None),
        P("dev", None),
        P(None, None, None, "dev"),
        P(None, "dev"),
        P("dev"),
        P(),
        P(None, "dev"),
        P(None, "dev"),
        P(None, "dev"),
        P(None, "dev"),
    )
    out_specs = (P(None, None, None, "dev"), P(None, None, None, "dev"))
    return jax.shard_map(
        functools.partial(shards, mesh.shape["dev"]),
        mesh=mesh,
        in_specs=in_specs,
        out_specs=out_specs,
        check_vma=False,
    )
```

```python
import functools

import jax
import jax.numpy as jnp
from jax import lax
from jax.experimental import pallas as pl
from jax.experimental.pallas import tpu as pltpu
from jax.sharding import PartitionSpec as P

F = 10
M = 7
E = 512
HALO = 256
PLACE = (0, 2, 4, 6, 1, 3, 5)
EVEN = (0, 2, 4, 6)
ODD = (1, 3, 5)
BLOCK = 8 * F
ROWS = M * BLOCK
NN = (((1,), (0,)), ((), ()))
NT = (((1,), (1,)), ((), ()))
F32 = jnp.float32
BF16 = jnp.bfloat16


def send_order(sizes):
    left = [
        (a, b, c, d)
        for d in range(sizes[3])
        for c in range(sizes[2])
        for b in range(sizes[1])
        for a in range(sizes[0])
    ][1:]

    def hops(offset):
        load = []
        for step, size in zip(offset[:3], sizes):
            back = size - step if step else 0
            load += [step * (step <= back), back * (back <= step)]
            if step and step == back:
                load[-2:] = [step / 2, back / 2]
        return load

    total = [0.0] * 6
    order = []
    while left:

        def score(offset):
            load = [a + b for a, b in zip(total, hops(offset))]
            even = max(load) - min(load) + 0.01 * sum(v * v for v in load) / (1 + sum(load))
            return even - 0.3 * sum(hops(offset))

        best = min(left, key=score)
        left.remove(best)
        order.append(best)
        total = [a + b for a, b in zip(total, hops(best))]
    return order


def iota(shape, dim):
    return lax.broadcasted_iota(jnp.int32, shape, dim)


def dot(a, b, dims=NN):
    return lax.dot_general(a, b, dims, preferred_element_type=F32)


def exact_dot(a, b, dims=NN):
    return lax.dot_general(
        a, b, dims, precision=lax.Precision.HIGHEST, preferred_element_type=F32
    )


def halves(value):
    high = value.astype(BF16)
    low = (value - high.astype(F32)).astype(BF16)
    return high, low


def one_hot(equal):
    return jnp.where(equal, 1.0, 0.0).astype(BF16)


def column(row):
    return jnp.transpose(jnp.broadcast_to(row.astype(F32), (8, row.shape[1])))[:, 0:1].astype(jnp.int32)


def build_operators(coup, even_ops, odd_ops):
    wide = 384
    r = iota((BLOCK, wide), 0)
    c = iota((BLOCK, wide), 1)
    at = (
        (c >= BLOCK).astype(jnp.int32)
        + (c >= 2 * BLOCK).astype(jnp.int32)
        + (c >= 3 * BLOCK).astype(jnp.int32)
        + (c >= 4 * BLOCK).astype(jnp.int32)
    )
    jr = r & 7
    jc = c & 7
    same_j = jr == jc
    even_sum = ((jr + jc) & 1) == 0
    two_jc = (2 * jc + 1).astype(F32)
    d_j = jnp.where((jc < jr) & ~even_sum, two_jc, 0.0)
    delta_j = jnp.where(same_j, 1.0, 0.0)
    pair_j = jnp.where(even_sum, 2.0, 0.0)
    parity_jc = jnp.where((jc & 1) == 0, 1.0, -1.0)

    spread_f = jnp.where((iota((BLOCK, F), 0) >> 3) == iota((BLOCK, F), 1), 1.0, 0.0)
    cg = iota((F, wide), 1)
    cg_at = (
        (cg >= BLOCK).astype(jnp.int32)
        + (cg >= 2 * BLOCK).astype(jnp.int32)
        + (cg >= 3 * BLOCK).astype(jnp.int32)
        + (cg >= 4 * BLOCK).astype(jnp.int32)
    )
    spread_g = jnp.where(((cg - cg_at * BLOCK) >> 3) == iota((F, wide), 0), 1.0, 0.0)
    c0, c1, c2, c3 = (
        exact_dot(exact_dot(spread_f, coup[:, k, :], NT), spread_g) for k in range(4)
    )

    def build(ops, own, other, store):
        first = own[0]
        valid = at < len(own)
        ic = 2 * at + first
        two_ic = (2 * ic + 1).astype(F32)
        zero = jnp.zeros((BLOCK, wide), F32)
        blocks = [
            jnp.where(valid, c3 * delta_j, zero),
            jnp.where(valid & (ic == jr), c3 * parity_jc, zero),
            jnp.where(valid & (ic == jr), c3, zero),
        ]
        for i in other:
            if i > 0:
                blocks.append(jnp.where(valid & (ic < i), c0 * delta_j * two_ic, zero))
        for i in own:
            blocks.append(jnp.where(valid & (ic == i), c1 * d_j, zero))
        for i in own:
            same_i = ic == i
            here = c3 * (2.0 * delta_j + jnp.where(same_i, pair_j, 0.0))
            here = here + jnp.where(same_i, c2 * delta_j, 0.0)
            blocks.append(jnp.where(valid, here, zero))
        for at_row, block in enumerate(blocks):
            store(ops, at_row * BLOCK, block)

    def store_even(ops, row, block):
        high = block.astype(BF16).astype(F32)
        low = block - high
        rows = pl.ds(row, BLOCK)
        ops[rows, 0:256] = high[:, 0:256].astype(BF16)
        shared = high[:, 256:384] + pltpu.roll(low[:, 256:384], 64, 1)
        ops[rows, 256:384] = shared.astype(BF16)
        ops[rows, 384:640] = low[:, 0:256].astype(BF16)
        ops[rows, 640:896] = high[:, 0:256].astype(BF16)
        ops[rows, 896:1024] = high[:, 256:384].astype(BF16)

    def store_odd(ops, row, block):
        high, low = halves(block[:, 0:256])
        rows = pl.ds(row, BLOCK)
        ops[rows, 0:256] = high
        ops[rows, 256:512] = low
        ops[rows, 512:768] = high

    build(even_ops, EVEN, ODD, store_even)
    build(odd_ops, ODD, EVEN, store_odd)


def residual_block(at, i, base, across, masks):
    odd_row = (iota((8, E), 0) & 1) == 1
    mask = masks[i]
    parts = []
    for f in range(F):
        plus = jnp.broadcast_to(across[0, pl.ds(8 * f + i, 1), :], (8, E))
        minus = jnp.broadcast_to(across[2, pl.ds(8 * f + i, 1), :], (8, E))
        lift = jnp.where(odd_row, minus, plus) + across[1 if i % 2 == 0 else 3, pl.ds(8 * f, 8), :]
        parts.append((base[pl.ds(BLOCK * at + 8 * f, 8), :] - lift) * mask)
    return jnp.concatenate(parts, axis=0)


def kernel(
    n,
    lam,
    order_far,
    send_far,
    recv_far,
    grad,
    metric_far,
    step_far,
    coup_far,
    neighbour_far,
    face_far,
    orient_far,
    halo_far,
    field,
    base,
    across,
    masks,
    pace_out,
    x_in,
    g_in,
    order,
    send_index,
    recv_slot,
    metric,
    step,
    coup,
    neighbour,
    neighbour_face,
    orient,
    halo_send,
    compact,
    send_buf,
    recv_buf,
    oh_slot,
    oh_local,
    oh_ghost,
    oh_halo,
    oh_halo_arrived,
    oh_local_arrived,
    even_ops,
    odd_ops,
    even_v,
    odd_v,
    traces,
    trace_halves,
    faces_send,
    faces_recv,
    halo_out,
    halo_in,
    even_res,
    odd_res,
    input_sem,
    local_sem,
    move_send,
    move_recv,
    face_send_sem,
    face_recv_sem,
    halo_send_sem,
    halo_recv_sem,
):
    me = lax.axis_index("dev")
    cap = E // n
    chunk = 4 * cap
    above = lax.rem(me + 1, n)
    below = lax.rem(me + n - 1, n)
    core = lax.rem(me, 2)
    far = jnp.where(core == 0, below, above)
    near = jnp.where(core == 0, above, below)
    barrier = pltpu.get_barrier_semaphore()

    fetches = [
        pltpu.make_async_copy(source, target, input_sem.at[at])
        for at, (source, target) in enumerate(
            (
                (send_far, send_index),
                (order_far, order),
                (lam, x_in),
                (neighbour_far, neighbour),
                (face_far, neighbour_face),
                (orient_far, orient),
                (halo_far, halo_send),
                (recv_far, recv_slot),
                (coup_far, coup),
                (metric_far, metric),
                (step_far, step),
                (grad, g_in),
            )
        )
    ]
    for fetch in fetches:
        fetch.start()

    sizes = (n // 32, 4, 4, 2) if n >= 32 else (1, 1, n // 2, 2)
    partners = []
    for offset in send_order(sizes):
        p = lax.rem(core + offset[3], 2)
        weight = 2
        place = me // 2
        for shift, size in zip(offset[2::-1], sizes[2::-1]):
            here = lax.rem(place, size)
            if shift:
                here = lax.rem(here + jnp.where(core == 0, shift, size - shift), size)
            p = p + weight * here
            weight = weight * size
            place = place // size
        partners.append(p)
    for p in partners:
        pl.semaphore_signal(barrier, inc=1, device_id=(p,), device_id_type=pl.DeviceIdType.MESH)

    fetches[0].wait()
    fetches[1].wait()
    oh_send = one_hot(column(send_index[...]) == iota((E, E), 1))
    tail = jnp.where(iota((E - F * M * M, E), 0) == 0, order[...].astype(F32), 0.0)
    compact[pl.ds(F * M * M, E - F * M * M), :] = tail
    fetches[2].wait()
    for at, i in enumerate(PLACE):
        for f in range(F):
            compact[pl.ds(M * (at * F + f), M), :] = x_in[f, i]
    high, low = halves(compact[...])
    sorted_rows = dot(oh_send, high, NT) + dot(oh_send, low, NT)
    for part in range(4):
        send_buf[pl.ds(part, E, stride=4), :] = sorted_rows[:, 128 * part : 128 * (part + 1)]

    for fetch in fetches[3:6]:
        fetch.wait()
    rows = iota((E, E), 0)
    for k in range(4):
        oh_ghost[:, E * k : E * (k + 1)] = one_hot(rows == ((neighbour[pl.ds(k, 1), :] - E) ^ (HALO * core)))
    wanted = jnp.zeros((16, E), F32)
    for k in range(4):
        code = neighbour_face[pl.ds(k, 1), :] + 4 * orient[pl.ds(k, 1), :]
        code = jnp.broadcast_to(code.astype(F32), (16, E)).astype(BF16)
        wanted = wanted + dot(code, oh_ghost[:, E * k : E * (k + 1)], NT)
    faces_send[0] = wanted[0:8, 0:HALO]
    faces_send[1] = wanted[0:8, HALO:E]
    tells = [
        pltpu.make_async_remote_copy(
            src_ref=faces_send.at[side],
            dst_ref=faces_recv.at[side],
            send_sem=face_send_sem.at[side],
            recv_sem=face_recv_sem.at[side],
            device_id=(whom,),
            device_id_type=pl.DeviceIdType.MESH,
        )
        for side, whom in enumerate((far, near))
    ]
    pl.semaphore_wait(barrier, n - 1)
    for tell in tells:
        tell.start()

    def piece(p):
        return pl.ds(pl.multiple_of(p * chunk, chunk), chunk)

    def send(p):
        pltpu.make_async_remote_copy(
            src_ref=send_buf.at[piece(p), :],
            dst_ref=recv_buf.at[piece(me), :],
            send_sem=move_send,
            recv_sem=move_recv,
            device_id=(p,),
            device_id_type=pl.DeviceIdType.MESH,
        ).start()

    for p in partners:
        send(p)
    own = pltpu.make_async_copy(send_buf.at[piece(me), :], recv_buf.at[piece(me), :], local_sem.at[0])
    own.start()

    for fetch in fetches[6:]:
        fetch.wait()
    for k in range(4):
        name = neighbour[pl.ds(k, 1), :]
        oh_local[:, E * k : E * (k + 1)] = one_hot(rows == name)
    for side in range(2):
        oh_halo[:, HALO * side : HALO * (side + 1)] = one_hot(
            iota((E, HALO), 0) == halo_send[pl.ds(core if side == 0 else 1 - core, 1), :]
        )

    south, east, north, west = (oh_ghost[:, E * k : E * (k + 1)].astype(F32) for k in range(4))
    for at, both in enumerate((north + south, east + west, north - south, east - west)):
        oh_ghost[:, E * at : E * (at + 1)] = both.astype(BF16)
    oh_slot[...] = one_hot(column(recv_slot[...]) == iota((E, E), 1))
    oh_halo_arrived[...] = dot(oh_slot[...], oh_halo[...]).astype(BF16)
    for k in range(4):
        lanes = slice(E * k, E * (k + 1))
        oh_local_arrived[:, lanes] = dot(oh_slot[...], oh_local[:, lanes]).astype(BF16)
    build_operators(coup, even_ops, odd_ops)
    even_v[pl.ds(960, 64), :] = jnp.zeros((64, E), BF16)
    base[...] = jnp.zeros((ROWS, E), F32)
    for part in range(3):
        odd_v[pl.ds(256 * part + 240, 16), :] = jnp.zeros((16, E), BF16)
    for tell in tells:
        tell.wait()

    own.wait()
    everyone = pl.ds(0, (n - 1) * chunk)
    arrived = pltpu.make_async_remote_copy(
        src_ref=send_buf.at[everyone, :],
        dst_ref=recv_buf.at[everyone, :],
        send_sem=move_send,
        recv_sem=move_recv,
        device_id=(above,),
        device_id_type=pl.DeviceIdType.MESH,
    )
    arrived.wait_recv()
    for part in range(4):
        compact[pl.ds(128 * part, 128), :] = jnp.transpose(recv_buf[pl.ds(part, E, stride=4), :])

    mode_j = iota((8, E), 0).astype(F32)

    def mode_masks(order_row):
        mask_j = jnp.where(mode_j <= order_row, 1.0, 0.0)
        return [jnp.where(order_row >= float(i), mask_j, 0.0) for i in range(M)]

    order_arrived = compact[pl.ds(F * M * M, 1), :]

    def keep_halves(at, value):
        high, low = halves(value)
        if at < 3:
            even_v[pl.ds(BLOCK * at, BLOCK), :] = high
        else:
            even_v[pl.ds(240, 16), :] = high[0:16]
            even_v[pl.ds(256, 64), :] = high[16:80]
            even_v[pl.ds(320, 64), :] = high[16:80]
        if at < 3:
            even_v[pl.ds(384 + BLOCK * at, BLOCK), :] = high
        else:
            even_v[pl.ds(384 + 240, 16), :] = high[0:16]
        even_v[pl.ds(640 + BLOCK * at, BLOCK), :] = low

    def keep_odd_halves(at, value):
        high, low = halves(value)
        odd_v[pl.ds(BLOCK * at, BLOCK), :] = high
        odd_v[pl.ds(256 + BLOCK * at, BLOCK), :] = high
        odd_v[pl.ds(512 + BLOCK * at, BLOCK), :] = low

    def place_block(at, value):
        if at < 4:
            keep_halves(at, value)
        else:
            keep_odd_halves(at - 4, value)

    masks_arrived = mode_masks(order_arrived)
    for at, i in enumerate(PLACE):
        parts = [compact[pl.ds(M * (at * F + f), 8), :] * masks_arrived[i] for f in range(F)]
        place_block(at, jnp.concatenate(parts, axis=0))

    def set_field(at, value):
        field[pl.ds(BLOCK * at, BLOCK), :] = value
        place_block(at, value)

    def take_slots():
        order_rows = jnp.broadcast_to(order_arrived, (16, E)).astype(BF16)
        order_row = dot(order_rows, oh_slot[...])[0:1]
        for i, mask in enumerate(mode_masks(order_row)):
            masks[i] = mask
        high = jnp.concatenate([even_v[pl.ds(0, 320), :], odd_v[pl.ds(0, 240), :]], axis=0)
        low = jnp.concatenate([even_v[pl.ds(640, 320), :], odd_v[pl.ds(512, 240), :]], axis=0)
        high = dot(high, oh_slot[...])
        low = dot(low, oh_slot[...])
        field[...] = high + low
        high = high.astype(BF16)
        low = low.astype(BF16)
        even_v[pl.ds(0, 320), :] = high[0:320]
        even_v[pl.ds(320, 64), :] = high[256:320]
        even_v[pl.ds(384, 256), :] = high[0:256]
        even_v[pl.ds(640, 320), :] = low[0:320]
        odd_v[pl.ds(0, 240), :] = high[320:560]
        odd_v[pl.ds(256, 240), :] = high[320:560]
        odd_v[pl.ds(512, 240), :] = low[320:560]

    odd_row = (iota((8, E), 0) & 1) == 1
    m0 = metric[pl.ds(0, 1), :]
    m1 = metric[pl.ds(1, 1), :]
    pace = step[...]

    pending = []

    def send_halo(sweep, chosen_halo):
        copies = []
        for side, whom in enumerate((far, near)):
            picked = dot(trace_halves[...], chosen_halo[:, HALO * side : HALO * (side + 1)])
            picked = picked[0:320] + picked[320:640]
            code = faces_recv[side][0:1, :]
            flipped = code >= 4.0
            face = jnp.where(flipped, code - 4.0, code)
            chosen = picked[240:320]
            for k in (2, 1, 0):
                chosen = jnp.where(face == float(k), picked[80 * k : 80 * (k + 1)], chosen)
            sign = jnp.where(odd_row[:, 0:HALO] & flipped, -1.0, 1.0)
            halo_out[sweep, side] = chosen * jnp.concatenate([sign] * F, axis=0)
            copies.append(
                pltpu.make_async_remote_copy(
                    src_ref=halo_out.at[sweep, side],
                    dst_ref=halo_in.at[sweep, side],
                    send_sem=halo_send_sem.at[sweep, side],
                    recv_sem=halo_recv_sem.at[sweep, side],
                    device_id=(whom,),
                    device_id_type=pl.DeviceIdType.MESH,
                )
            )
            copies[-1].start()
        return copies

    def turned(k):
        sign = jnp.where(odd_row & (orient[pl.ds(k, 1), :] == 1), -1.0, 1.0)
        return jnp.concatenate([sign] * F, axis=0)

    def combine(across):
        south = across[0]
        north = across[2]
        across[0] = north + south
        across[2] = north - south
        east = across[1]
        west = across[3]
        across[1] = east + west
        across[3] = east - west

    def residual(sweep, chosen_halo, chosen_local, before_volume, finish):
        from_even = dot(even_ops[pl.ds(0, 240), :], even_v[...])
        from_odd = dot(odd_ops[pl.ds(0, 240), :], odd_v[...])
        traces[0] = from_even[80:160] + from_odd[80:160]
        traces[1] = from_even[0:80] + from_odd[0:80]
        traces[2] = from_even[160:240] + from_odd[160:240]
        traces[3] = from_even[0:80] - from_odd[0:80]
        for k in range(4):
            high, low = halves(traces[k])
            trace_halves[pl.ds(80 * k, 80), :] = high
            trace_halves[pl.ds(320 + 80 * k, 80), :] = low
        sent = send_halo(sweep, chosen_halo)
        pending.extend(sent)

        for k in range(4):
            got = dot(trace_halves[...], chosen_local[:, E * k : E * (k + 1)])
            got = got[0:320] + got[320:640]
            face = neighbour_face[pl.ds(k, 1), :]
            chosen = got[240:320]
            for other in (2, 1, 0):
                chosen = jnp.where(face == other, got[80 * other : 80 * (other + 1)], chosen)
            across[k] = chosen * turned(k)
        combine(across)
        before_volume()
        even_res[...] = dot(even_ops[pl.ds(240, 880), :], even_v[...])
        odd_res[...] = dot(odd_ops[pl.ds(240, 720), :], odd_v[...])

        for at, i in enumerate(PLACE):
            if i % 2 == 0:
                here = m1 * even_res[pl.ds(240 + BLOCK * at, BLOCK), :]
                here = here + even_res[pl.ds(560 + BLOCK * at, BLOCK), :]
                if i > 0:
                    here = here + m0 * odd_res[pl.ds(BLOCK * (at - 1), BLOCK), :]
            else:
                here = m1 * odd_res[pl.ds(240 + BLOCK * (at - 4), BLOCK), :]
                here = here + odd_res[pl.ds(480 + BLOCK * (at - 4), BLOCK), :]
                here = here + m0 * even_res[pl.ds(BLOCK * (at - 4), BLOCK), :]
            for f in range(F):
                base[pl.ds(BLOCK * at + 8 * f, M), :] = here[8 * f : 8 * f + M] - g_in[f, i]

        for side in (1, 0):
            sent[side].wait_recv()
            ghost_halves = jnp.concatenate(list(halves(halo_in[sweep, side])), axis=0)
            for at in range(4):
                got = dot(ghost_halves, oh_ghost[HALO * side : HALO * (side + 1), E * at : E * (at + 1)])
                across[at] = across[at] + (got[0:80] + got[80:160])

        finish()

    def next_field():
        for at, i in enumerate(PLACE):
            value = residual_block(at, i, base, across, masks)
            set_field(at, field[pl.ds(BLOCK * at, BLOCK), :] - pace * value)

    residual(0, oh_halo_arrived, oh_local_arrived, take_slots, next_field)
    residual(1, oh_halo, oh_local, lambda: None, lambda: None)
    pace_out[...] = pace
    arrived.wait_send()
    for copy in pending:
        copy.wait_send()


def last_step(field, base, across, masks, pace, out_two, out_res, two, res, sem):
    copies = []
    for at, i in enumerate(PLACE):
        value = residual_block(at, i, base, across, masks)
        advanced = field[pl.ds(BLOCK * at, BLOCK), :] - pace[...] * value
        for f in range(F):
            res[f, i] = value[8 * f : 8 * f + M]
            two[f, i] = advanced[8 * f : 8 * f + M]
        for kind, (near, far) in enumerate(((two, out_two), (res, out_res))):
            copies.append(pltpu.make_async_copy(near.at[:, i], far.at[:, i], sem.at[kind, i]))
            copies[-1].start()
    for copy in copies:
        copy.wait()


def shards(n, *args):
    (lam, order, send_index, recv_slot, grad, metric, step, coup, neighbour, neighbour_face, orient, halo_send) = args
    anywhere = pl.BlockSpec(memory_space=pl.ANY)
    shape = jax.ShapeDtypeStruct((F, M, M, E), F32)
    kept = pl.pallas_call(
        functools.partial(kernel, n),
        out_shape=(
            pltpu.VMEM((ROWS, E), F32),
            pltpu.VMEM((ROWS, E), F32),
            pltpu.VMEM((4, BLOCK, E), F32),
            pltpu.VMEM((M, 8, E), F32),
            pltpu.VMEM((1, E), F32),
        ),
        in_specs=[pl.BlockSpec(memory_space=pltpu.HBM)] * 12,
        out_specs=(pl.BlockSpec(memory_space=pltpu.VMEM),) * 5,
        scratch_shapes=[
            pltpu.VMEM((F, M, M, E), F32),
            pltpu.VMEM((F, M, M, E), F32),
            pltpu.VMEM((1, E), jnp.int32),
            pltpu.VMEM((1, E), jnp.int32),
            pltpu.VMEM((1, E), jnp.int32),
            pltpu.VMEM((2, E), F32),
            pltpu.VMEM((1, E), F32),
            pltpu.VMEM((F, 4, F), F32),
            pltpu.VMEM((4, E), jnp.int32),
            pltpu.VMEM((4, E), jnp.int32),
            pltpu.VMEM((4, E), jnp.int32),
            pltpu.VMEM((2, HALO), jnp.int32),
            pltpu.VMEM((E, E), F32),
            pltpu.VMEM((4 * E, 128), F32),
            pltpu.VMEM((4 * E, 128), F32),
            pltpu.VMEM((E, E), BF16),
            pltpu.VMEM((E, 4 * E), BF16),
            pltpu.VMEM((E, 4 * E), BF16),
            pltpu.VMEM((E, E), BF16),
            pltpu.VMEM((E, E), BF16),
            pltpu.VMEM((E, 4 * E), BF16),
            pltpu.VMEM((14 * BLOCK, 1024), BF16),
            pltpu.VMEM((12 * BLOCK, 768), BF16),
            pltpu.VMEM((1024, E), BF16),
            pltpu.VMEM((768, E), BF16),
            pltpu.VMEM((4, BLOCK, E), F32),
            pltpu.VMEM((8 * BLOCK, E), BF16),
            pltpu.VMEM((2, 8, HALO), F32),
            pltpu.VMEM((2, 8, HALO), F32),
            pltpu.VMEM((2, 2, BLOCK, HALO), F32),
            pltpu.VMEM((2, 2, BLOCK, HALO), F32),
            pltpu.VMEM((11 * BLOCK, E), F32),
            pltpu.VMEM((9 * BLOCK, E), F32),
            pltpu.SemaphoreType.DMA((12,)),
            pltpu.SemaphoreType.DMA((1,)),
            pltpu.SemaphoreType.DMA,
            pltpu.SemaphoreType.DMA,
            pltpu.SemaphoreType.DMA((2,)),
            pltpu.SemaphoreType.DMA((2,)),
            pltpu.SemaphoreType.DMA((2, 2)),
            pltpu.SemaphoreType.DMA((2, 2)),
        ],
        compiler_params=pltpu.CompilerParams(
            collective_id=0, has_side_effects=True, vmem_limit_bytes=60928 * 1024
        ),
    )(
        lam,
        order.reshape(1, E),
        send_index,
        recv_slot,
        grad,
        metric,
        step.reshape(1, E),
        jnp.transpose(coup, (1, 0, 2)),
        neighbour,
        neighbour_face,
        orient,
        halo_send,
    )
    return pl.pallas_call(
        last_step,
        out_shape=(shape, shape),
        in_specs=[pl.BlockSpec(memory_space=pltpu.VMEM)] * 5,
        out_specs=(anywhere, anywhere),
        scratch_shapes=[
            pltpu.VMEM((F, M, M, E), F32),
            pltpu.VMEM((F, M, M, E), F32),
            pltpu.SemaphoreType.DMA((2, M)),
        ],
        compiler_params=pltpu.CompilerParams(vmem_limit_bytes=4 * 1024 * 1024),
    )(*kept)


def solution(mesh):
    in_specs = (
        P(None, None, None, "dev"),
        P("dev"),
        P("dev", None),
        P("dev", None),
        P(None, None, None, "dev"),
        P(None, "dev"),
        P("dev"),
        P(),
        P(None, "dev"),
        P(None, "dev"),
        P(None, "dev"),
        P(None, "dev"),
    )
    out_specs = (P(None, None, None, "dev"), P(None, None, None, "dev"))
    return jax.shard_map(
        functools.partial(shards, mesh.shape["dev"]),
        mesh=mesh,
        in_specs=in_specs,
        out_specs=out_specs,
        check_vma=False,
    )
```

```python
import functools

import jax
import jax.numpy as jnp
from jax import lax
from jax.experimental import pallas as pl
from jax.experimental.pallas import tpu as pltpu
from jax.sharding import PartitionSpec as P

F = 10
M = 7
E = 512
HALO = 256
PLACE = (0, 2, 4, 6, 1, 3, 5)
EVEN = (0, 2, 4, 6)
ODD = (1, 3, 5)
BLOCK = 8 * F
ROWS = M * BLOCK
NN = (((1,), (0,)), ((), ()))
NT = (((1,), (1,)), ((), ()))
F32 = jnp.float32
BF16 = jnp.bfloat16


def send_order(sizes):
    left = [
        (a, b, c, d)
        for d in range(sizes[3])
        for c in range(sizes[2])
        for b in range(sizes[1])
        for a in range(sizes[0])
    ][1:]

    def hops(offset):
        load = []
        for step, size in zip(offset[:3], sizes):
            back = size - step if step else 0
            load += [step * (step <= back), back * (back <= step)]
            if step and step == back:
                load[-2:] = [step / 2, back / 2]
        return load

    total = [0.0] * 6
    order = []
    while left:

        def score(offset):
            load = [a + b for a, b in zip(total, hops(offset))]
            even = max(load) - min(load) + 0.01 * sum(v * v for v in load) / (1 + sum(load))
            return even - 0.3 * sum(hops(offset))

        best = min(left, key=score)
        left.remove(best)
        order.append(best)
        total = [a + b for a, b in zip(total, hops(best))]
    return order


def iota(shape, dim):
    return lax.broadcasted_iota(jnp.int32, shape, dim)


def dot(a, b, dims=NN):
    return lax.dot_general(a, b, dims, preferred_element_type=F32)


def exact_dot(a, b, dims=NN):
    return lax.dot_general(
        a, b, dims, precision=lax.Precision.HIGHEST, preferred_element_type=F32
    )


def halves(value):
    high = value.astype(BF16)
    low = (value - high.astype(F32)).astype(BF16)
    return high, low


def one_hot(equal):
    return jnp.where(equal, 1.0, 0.0).astype(BF16)


def column(row):
    return jnp.transpose(jnp.broadcast_to(row.astype(F32), (8, row.shape[1])))[:, 0:1].astype(jnp.int32)


def build_operators(coup, even_ops, odd_ops):
    wide = 384
    r = iota((BLOCK, wide), 0)
    c = iota((BLOCK, wide), 1)
    at = (
        (c >= BLOCK).astype(jnp.int32)
        + (c >= 2 * BLOCK).astype(jnp.int32)
        + (c >= 3 * BLOCK).astype(jnp.int32)
        + (c >= 4 * BLOCK).astype(jnp.int32)
    )
    jr = r & 7
    jc = c & 7
    same_j = jr == jc
    even_sum = ((jr + jc) & 1) == 0
    two_jc = (2 * jc + 1).astype(F32)
    d_j = jnp.where((jc < jr) & ~even_sum, two_jc, 0.0)
    delta_j = jnp.where(same_j, 1.0, 0.0)
    pair_j = jnp.where(even_sum, 2.0, 0.0)
    parity_jc = jnp.where((jc & 1) == 0, 1.0, -1.0)

    spread_f = jnp.where((iota((BLOCK, F), 0) >> 3) == iota((BLOCK, F), 1), 1.0, 0.0)
    cg = iota((F, wide), 1)
    cg_at = (
        (cg >= BLOCK).astype(jnp.int32)
        + (cg >= 2 * BLOCK).astype(jnp.int32)
        + (cg >= 3 * BLOCK).astype(jnp.int32)
        + (cg >= 4 * BLOCK).astype(jnp.int32)
    )
    spread_g = jnp.where(((cg - cg_at * BLOCK) >> 3) == iota((F, wide), 0), 1.0, 0.0)
    c0, c1, c2, c3 = (
        exact_dot(exact_dot(spread_f, coup[:, k, :], NT), spread_g) for k in range(4)
    )

    def build(ops, own, other, store):
        first = own[0]
        valid = at < len(own)
        ic = 2 * at + first
        two_ic = (2 * ic + 1).astype(F32)
        zero = jnp.zeros((BLOCK, wide), F32)
        blocks = [
            jnp.where(valid, c3 * delta_j, zero),
            jnp.where(valid & (ic == jr), c3 * parity_jc, zero),
            jnp.where(valid & (ic == jr), c3, zero),
        ]
        for i in other:
            if i > 0:
                blocks.append(jnp.where(valid & (ic < i), c0 * delta_j * two_ic, zero))
        for i in own:
            blocks.append(jnp.where(valid & (ic == i), c1 * d_j, zero))
        for i in own:
            same_i = ic == i
            here = c3 * (2.0 * delta_j + jnp.where(same_i, pair_j, 0.0))
            here = here + jnp.where(same_i, c2 * delta_j, 0.0)
            blocks.append(jnp.where(valid, here, zero))
        for at_row, block in enumerate(blocks):
            store(ops, at_row * BLOCK, block)

    def store_even(ops, row, block):
        high = block.astype(BF16).astype(F32)
        low = block - high
        rows = pl.ds(row, BLOCK)
        ops[rows, 0:256] = high[:, 0:256].astype(BF16)
        shared = high[:, 256:384] + pltpu.roll(low[:, 256:384], 64, 1)
        ops[rows, 256:384] = shared.astype(BF16)
        ops[rows, 384:640] = low[:, 0:256].astype(BF16)
        ops[rows, 640:896] = high[:, 0:256].astype(BF16)
        ops[rows, 896:1024] = high[:, 256:384].astype(BF16)

    def store_odd(ops, row, block):
        high, low = halves(block[:, 0:256])
        rows = pl.ds(row, BLOCK)
        ops[rows, 0:256] = high
        ops[rows, 256:512] = low
        ops[rows, 512:768] = high

    build(even_ops, EVEN, ODD, store_even)
    build(odd_ops, ODD, EVEN, store_odd)


def residual_block(at, i, base, across, masks):
    odd_row = (iota((8, E), 0) & 1) == 1
    mask = masks[i]
    parts = []
    for f in range(F):
        plus = jnp.broadcast_to(across[0, pl.ds(8 * f + i, 1), :], (8, E))
        minus = jnp.broadcast_to(across[2, pl.ds(8 * f + i, 1), :], (8, E))
        lift = jnp.where(odd_row, minus, plus) + across[1 if i % 2 == 0 else 3, pl.ds(8 * f, 8), :]
        parts.append((base[pl.ds(BLOCK * at + 8 * f, 8), :] - lift) * mask)
    return jnp.concatenate(parts, axis=0)


def kernel(
    n,
    lam,
    order_far,
    send_far,
    recv_far,
    grad,
    metric_far,
    step_far,
    coup_far,
    neighbour_far,
    face_far,
    orient_far,
    halo_far,
    field,
    base,
    across,
    masks,
    pace_out,
    x_in,
    g_in,
    order,
    send_index,
    recv_slot,
    metric,
    step,
    coup,
    neighbour,
    neighbour_face,
    orient,
    halo_send,
    compact,
    send_buf,
    recv_buf,
    oh_slot,
    oh_local,
    oh_ghost,
    oh_halo,
    oh_halo_arrived,
    oh_local_arrived,
    even_ops,
    odd_ops,
    even_v,
    odd_v,
    traces,
    trace_halves,
    faces_send,
    faces_recv,
    halo_out,
    halo_in,
    even_res,
    odd_res,
    input_sem,
    local_sem,
    move_send,
    move_recv,
    face_send_sem,
    face_recv_sem,
    halo_send_sem,
    halo_recv_sem,
):
    me = lax.axis_index("dev")
    cap = E // n
    chunk = 4 * cap
    above = lax.rem(me + 1, n)
    below = lax.rem(me + n - 1, n)
    core = lax.rem(me, 2)
    far = jnp.where(core == 0, below, above)
    near = jnp.where(core == 0, above, below)
    barrier = pltpu.get_barrier_semaphore()

    fetches = [
        pltpu.make_async_copy(source, target, input_sem.at[at])
        for at, (source, target) in enumerate(
            (
                (send_far, send_index),
                (order_far, order),
                (lam, x_in),
                (neighbour_far, neighbour),
                (face_far, neighbour_face),
                (orient_far, orient),
                (halo_far, halo_send),
                (recv_far, recv_slot),
                (coup_far, coup),
                (metric_far, metric),
                (step_far, step),
                (grad, g_in),
            )
        )
    ]
    for fetch in fetches:
        fetch.start()

    sizes = (n // 32, 4, 4, 2) if n >= 32 else (1, 1, n // 2, 2)
    partners = []
    for offset in send_order(sizes):
        p = lax.rem(core + offset[3], 2)
        weight = 2
        place = me // 2
        for shift, size in zip(offset[2::-1], sizes[2::-1]):
            here = lax.rem(place, size)
            if shift:
                here = lax.rem(here + jnp.where(core == 0, shift, size - shift), size)
            p = p + weight * here
            weight = weight * size
            place = place // size
        partners.append(p)
    for p in partners:
        pl.semaphore_signal(barrier, inc=1, device_id=(p,), device_id_type=pl.DeviceIdType.MESH)

    fetches[0].wait()
    fetches[1].wait()
    oh_send = one_hot(column(send_index[...]) == iota((E, E), 1))
    tail = jnp.where(iota((E - F * M * M, E), 0) == 0, order[...].astype(F32), 0.0)
    compact[pl.ds(F * M * M, E - F * M * M), :] = tail
    fetches[2].wait()
    for at, i in enumerate(PLACE):
        for f in range(F):
            compact[pl.ds(M * (at * F + f), M), :] = x_in[f, i]
    high, low = halves(compact[...])
    sorted_rows = dot(oh_send, high, NT) + dot(oh_send, low, NT)
    for part in range(4):
        send_buf[pl.ds(part, E, stride=4), :] = sorted_rows[:, 128 * part : 128 * (part + 1)]

    for fetch in fetches[3:6]:
        fetch.wait()
    rows = iota((E, E), 0)
    for k in range(4):
        oh_ghost[:, E * k : E * (k + 1)] = one_hot(rows == ((neighbour[pl.ds(k, 1), :] - E) ^ (HALO * core)))
    wanted = jnp.zeros((16, E), F32)
    for k in range(4):
        code = neighbour_face[pl.ds(k, 1), :] + 4 * orient[pl.ds(k, 1), :]
        code = jnp.broadcast_to(code.astype(F32), (16, E)).astype(BF16)
        wanted = wanted + dot(code, oh_ghost[:, E * k : E * (k + 1)], NT)
    faces_send[0] = wanted[0:8, 0:HALO]
    faces_send[1] = wanted[0:8, HALO:E]
    tells = [
        pltpu.make_async_remote_copy(
            src_ref=faces_send.at[side],
            dst_ref=faces_recv.at[side],
            send_sem=face_send_sem.at[side],
            recv_sem=face_recv_sem.at[side],
            device_id=(whom,),
            device_id_type=pl.DeviceIdType.MESH,
        )
        for side, whom in enumerate((far, near))
    ]
    pl.semaphore_wait(barrier, n - 1)
    for tell in tells:
        tell.start()

    def piece(p):
        return pl.ds(pl.multiple_of(p * chunk, chunk), chunk)

    def send(p):
        pltpu.make_async_remote_copy(
            src_ref=send_buf.at[piece(p), :],
            dst_ref=recv_buf.at[piece(me), :],
            send_sem=move_send,
            recv_sem=move_recv,
            device_id=(p,),
            device_id_type=pl.DeviceIdType.MESH,
        ).start()

    for p in partners:
        send(p)
    own = pltpu.make_async_copy(send_buf.at[piece(me), :], recv_buf.at[piece(me), :], local_sem.at[0])
    own.start()

    for fetch in fetches[6:]:
        fetch.wait()
    for k in range(4):
        name = neighbour[pl.ds(k, 1), :]
        oh_local[:, E * k : E * (k + 1)] = one_hot(rows == name)
    for side in range(2):
        oh_halo[:, HALO * side : HALO * (side + 1)] = one_hot(
            iota((E, HALO), 0) == halo_send[pl.ds(core if side == 0 else 1 - core, 1), :]
        )

    south, east, north, west = (oh_ghost[:, E * k : E * (k + 1)].astype(F32) for k in range(4))
    for at, both in enumerate((north + south, east + west, north - south, east - west)):
        oh_ghost[:, E * at : E * (at + 1)] = both.astype(BF16)
    oh_slot[...] = one_hot(column(recv_slot[...]) == iota((E, E), 1))
    oh_halo_arrived[...] = dot(oh_slot[...], oh_halo[...]).astype(BF16)
    for k in range(4):
        lanes = slice(E * k, E * (k + 1))
        oh_local_arrived[:, lanes] = dot(oh_slot[...], oh_local[:, lanes]).astype(BF16)
    build_operators(coup, even_ops, odd_ops)
    even_v[pl.ds(960, 64), :] = jnp.zeros((64, E), BF16)
    base[...] = jnp.zeros((ROWS, E), F32)
    for part in range(3):
        odd_v[pl.ds(256 * part + 240, 16), :] = jnp.zeros((16, E), BF16)
    for tell in tells:
        tell.wait()

    own.wait()
    everyone = pl.ds(0, (n - 1) * chunk)
    arrived = pltpu.make_async_remote_copy(
        src_ref=send_buf.at[everyone, :],
        dst_ref=recv_buf.at[everyone, :],
        send_sem=move_send,
        recv_sem=move_recv,
        device_id=(above,),
        device_id_type=pl.DeviceIdType.MESH,
    )
    arrived.wait_recv()
    for part in range(4):
        compact[pl.ds(128 * part, 128), :] = jnp.transpose(recv_buf[pl.ds(part, E, stride=4), :])

    mode_j = iota((8, E), 0).astype(F32)

    def mode_masks(order_row):
        mask_j = jnp.where(mode_j <= order_row, 1.0, 0.0)
        return [jnp.where(order_row >= float(i), mask_j, 0.0) for i in range(M)]

    order_arrived = compact[pl.ds(F * M * M, 1), :]

    def keep_halves(at, value):
        high, low = halves(value)
        if at < 3:
            even_v[pl.ds(BLOCK * at, BLOCK), :] = high
        else:
            even_v[pl.ds(240, 16), :] = high[0:16]
            even_v[pl.ds(256, 64), :] = high[16:80]
            even_v[pl.ds(320, 64), :] = high[16:80]
        if at < 3:
            even_v[pl.ds(384 + BLOCK * at, BLOCK), :] = high
        else:
            even_v[pl.ds(384 + 240, 16), :] = high[0:16]
        even_v[pl.ds(640 + BLOCK * at, BLOCK), :] = low

    def keep_odd_halves(at, value):
        high, low = halves(value)
        odd_v[pl.ds(BLOCK * at, BLOCK), :] = high
        odd_v[pl.ds(256 + BLOCK * at, BLOCK), :] = high
        odd_v[pl.ds(512 + BLOCK * at, BLOCK), :] = low

    def place_block(at, value):
        if at < 4:
            keep_halves(at, value)
        else:
            keep_odd_halves(at - 4, value)

    masks_arrived = mode_masks(order_arrived)
    for at, i in enumerate(PLACE):
        parts = [compact[pl.ds(M * (at * F + f), 8), :] * masks_arrived[i] for f in range(F)]
        place_block(at, jnp.concatenate(parts, axis=0))

    def keep_field():
        for at in range(M):
            rows = pl.ds(BLOCK * at if at < 4 else BLOCK * (at - 4), BLOCK)
            low_rows = pl.ds(640 + BLOCK * at if at < 4 else 512 + BLOCK * (at - 4), BLOCK)
            source = even_v if at < 4 else odd_v
            field[pl.ds(BLOCK * at, BLOCK), :] = source[rows, :].astype(F32) + source[low_rows, :].astype(F32)

    def take_slots():
        order_rows = jnp.broadcast_to(order_arrived, (16, E)).astype(BF16)
        order_row = dot(order_rows, oh_slot[...])[0:1]
        for i, mask in enumerate(mode_masks(order_row)):
            masks[i] = mask
        high = jnp.concatenate([even_v[pl.ds(0, 320), :], odd_v[pl.ds(0, 240), :]], axis=0)
        low = jnp.concatenate([even_v[pl.ds(640, 320), :], odd_v[pl.ds(512, 240), :]], axis=0)
        high = dot(high, oh_slot[...])
        low = dot(low, oh_slot[...])
        field[...] = high + low
        high = high.astype(BF16)
        low = low.astype(BF16)
        even_v[pl.ds(0, 320), :] = high[0:320]
        even_v[pl.ds(320, 64), :] = high[256:320]
        even_v[pl.ds(384, 256), :] = high[0:256]
        even_v[pl.ds(640, 320), :] = low[0:320]
        odd_v[pl.ds(0, 240), :] = high[320:560]
        odd_v[pl.ds(256, 240), :] = high[320:560]
        odd_v[pl.ds(512, 240), :] = low[320:560]

    odd_row = (iota((8, E), 0) & 1) == 1
    m0 = metric[pl.ds(0, 1), :]
    m1 = metric[pl.ds(1, 1), :]
    pace = step[...]

    pending = []

    def send_halo(sweep, chosen_halo):
        copies = []
        for side, whom in enumerate((far, near)):
            picked = dot(trace_halves[...], chosen_halo[:, HALO * side : HALO * (side + 1)])
            picked = picked[0:320] + picked[320:640]
            code = faces_recv[side][0:1, :]
            flipped = code >= 4.0
            face = jnp.where(flipped, code - 4.0, code)
            chosen = picked[240:320]
            for k in (2, 1, 0):
                chosen = jnp.where(face == float(k), picked[80 * k : 80 * (k + 1)], chosen)
            sign = jnp.where(odd_row[:, 0:HALO] & flipped, -1.0, 1.0)
            halo_out[sweep, side] = chosen * jnp.concatenate([sign] * F, axis=0)
            copies.append(
                pltpu.make_async_remote_copy(
                    src_ref=halo_out.at[sweep, side],
                    dst_ref=halo_in.at[sweep, side],
                    send_sem=halo_send_sem.at[sweep, side],
                    recv_sem=halo_recv_sem.at[sweep, side],
                    device_id=(whom,),
                    device_id_type=pl.DeviceIdType.MESH,
                )
            )
            copies[-1].start()
        return copies

    def turned(k):
        sign = jnp.where(odd_row & (orient[pl.ds(k, 1), :] == 1), -1.0, 1.0)
        return jnp.concatenate([sign] * F, axis=0)

    def combine(across):
        south = across[0]
        north = across[2]
        across[0] = north + south
        across[2] = north - south
        east = across[1]
        west = across[3]
        across[1] = east + west
        across[3] = east - west

    def residual(sweep, chosen_halo, chosen_local, before_volume, finish):
        from_even = dot(even_ops[pl.ds(0, 240), :], even_v[...])
        from_odd = dot(odd_ops[pl.ds(0, 240), :], odd_v[...])
        traces[0] = from_even[80:160] + from_odd[80:160]
        traces[1] = from_even[0:80] + from_odd[0:80]
        traces[2] = from_even[160:240] + from_odd[160:240]
        traces[3] = from_even[0:80] - from_odd[0:80]
        for k in range(4):
            high, low = halves(traces[k])
            trace_halves[pl.ds(80 * k, 80), :] = high
            trace_halves[pl.ds(320 + 80 * k, 80), :] = low
        sent = send_halo(sweep, chosen_halo)
        pending.extend(sent)

        for k in range(4):
            got = dot(trace_halves[...], chosen_local[:, E * k : E * (k + 1)])
            got = got[0:320] + got[320:640]
            face = neighbour_face[pl.ds(k, 1), :]
            chosen = got[240:320]
            for other in (2, 1, 0):
                chosen = jnp.where(face == other, got[80 * other : 80 * (other + 1)], chosen)
            across[k] = chosen * turned(k)
        combine(across)
        before_volume()
        even_res[...] = dot(even_ops[pl.ds(240, 880), :], even_v[...])
        odd_res[...] = dot(odd_ops[pl.ds(240, 720), :], odd_v[...])

        for at, i in enumerate(PLACE):
            if i % 2 == 0:
                here = m1 * even_res[pl.ds(240 + BLOCK * at, BLOCK), :]
                here = here + even_res[pl.ds(560 + BLOCK * at, BLOCK), :]
                if i > 0:
                    here = here + m0 * odd_res[pl.ds(BLOCK * (at - 1), BLOCK), :]
            else:
                here = m1 * odd_res[pl.ds(240 + BLOCK * (at - 4), BLOCK), :]
                here = here + odd_res[pl.ds(480 + BLOCK * (at - 4), BLOCK), :]
                here = here + m0 * even_res[pl.ds(BLOCK * (at - 4), BLOCK), :]
            for f in range(F):
                base[pl.ds(BLOCK * at + 8 * f, M), :] = here[8 * f : 8 * f + M] - g_in[f, i]

        for side in (1, 0):
            sent[side].wait_recv()
            ghost_halves = jnp.concatenate(list(halves(halo_in[sweep, side])), axis=0)
            for at in range(4):
                got = dot(ghost_halves, oh_ghost[HALO * side : HALO * (side + 1), E * at : E * (at + 1)])
                across[at] = across[at] + (got[0:80] + got[80:160])

        finish()

    def next_field():
        for at, i in enumerate(PLACE):
            value = residual_block(at, i, base, across, masks)
            place_block(at, field[pl.ds(BLOCK * at, BLOCK), :] - pace * value)

    residual(0, oh_halo_arrived, oh_local_arrived, take_slots, next_field)
    residual(1, oh_halo, oh_local, keep_field, lambda: None)
    pace_out[...] = pace
    arrived.wait_send()
    for copy in pending:
        copy.wait_send()


def last_step(field, base, across, masks, pace, out_two, out_res, two, res, sem):
    copies = []
    for at, i in enumerate(PLACE):
        value = residual_block(at, i, base, across, masks)
        advanced = field[pl.ds(BLOCK * at, BLOCK), :] - pace[...] * value
        for f in range(F):
            res[f, i] = value[8 * f : 8 * f + M]
            two[f, i] = advanced[8 * f : 8 * f + M]
        for kind, (near, far) in enumerate(((two, out_two), (res, out_res))):
            copies.append(pltpu.make_async_copy(near.at[:, i], far.at[:, i], sem.at[kind, i]))
            copies[-1].start()
    for copy in copies:
        copy.wait()


def shards(n, *args):
    (lam, order, send_index, recv_slot, grad, metric, step, coup, neighbour, neighbour_face, orient, halo_send) = args
    anywhere = pl.BlockSpec(memory_space=pl.ANY)
    shape = jax.ShapeDtypeStruct((F, M, M, E), F32)
    kept = pl.pallas_call(
        functools.partial(kernel, n),
        out_shape=(
            pltpu.VMEM((ROWS, E), F32),
            pltpu.VMEM((ROWS, E), F32),
            pltpu.VMEM((4, BLOCK, E), F32),
            pltpu.VMEM((M, 8, E), F32),
            pltpu.VMEM((1, E), F32),
        ),
        in_specs=[pl.BlockSpec(memory_space=pltpu.HBM)] * 12,
        out_specs=(pl.BlockSpec(memory_space=pltpu.VMEM),) * 5,
        scratch_shapes=[
            pltpu.VMEM((F, M, M, E), F32),
            pltpu.VMEM((F, M, M, E), F32),
            pltpu.VMEM((1, E), jnp.int32),
            pltpu.VMEM((1, E), jnp.int32),
            pltpu.VMEM((1, E), jnp.int32),
            pltpu.VMEM((2, E), F32),
            pltpu.VMEM((1, E), F32),
            pltpu.VMEM((F, 4, F), F32),
            pltpu.VMEM((4, E), jnp.int32),
            pltpu.VMEM((4, E), jnp.int32),
            pltpu.VMEM((4, E), jnp.int32),
            pltpu.VMEM((2, HALO), jnp.int32),
            pltpu.VMEM((E, E), F32),
            pltpu.VMEM((4 * E, 128), F32),
            pltpu.VMEM((4 * E, 128), F32),
            pltpu.VMEM((E, E), BF16),
            pltpu.VMEM((E, 4 * E), BF16),
            pltpu.VMEM((E, 4 * E), BF16),
            pltpu.VMEM((E, E), BF16),
            pltpu.VMEM((E, E), BF16),
            pltpu.VMEM((E, 4 * E), BF16),
            pltpu.VMEM((14 * BLOCK, 1024), BF16),
            pltpu.VMEM((12 * BLOCK, 768), BF16),
            pltpu.VMEM((1024, E), BF16),
            pltpu.VMEM((768, E), BF16),
            pltpu.VMEM((4, BLOCK, E), F32),
            pltpu.VMEM((8 * BLOCK, E), BF16),
            pltpu.VMEM((2, 8, HALO), F32),
            pltpu.VMEM((2, 8, HALO), F32),
            pltpu.VMEM((2, 2, BLOCK, HALO), F32),
            pltpu.VMEM((2, 2, BLOCK, HALO), F32),
            pltpu.VMEM((11 * BLOCK, E), F32),
            pltpu.VMEM((9 * BLOCK, E), F32),
            pltpu.SemaphoreType.DMA((12,)),
            pltpu.SemaphoreType.DMA((1,)),
            pltpu.SemaphoreType.DMA,
            pltpu.SemaphoreType.DMA,
            pltpu.SemaphoreType.DMA((2,)),
            pltpu.SemaphoreType.DMA((2,)),
            pltpu.SemaphoreType.DMA((2, 2)),
            pltpu.SemaphoreType.DMA((2, 2)),
        ],
        compiler_params=pltpu.CompilerParams(
            collective_id=0, has_side_effects=True, vmem_limit_bytes=60928 * 1024
        ),
    )(
        lam,
        order.reshape(1, E),
        send_index,
        recv_slot,
        grad,
        metric,
        step.reshape(1, E),
        jnp.transpose(coup, (1, 0, 2)),
        neighbour,
        neighbour_face,
        orient,
        halo_send,
    )
    return pl.pallas_call(
        last_step,
        out_shape=(shape, shape),
        in_specs=[pl.BlockSpec(memory_space=pltpu.VMEM)] * 5,
        out_specs=(anywhere, anywhere),
        scratch_shapes=[
            pltpu.VMEM((F, M, M, E), F32),
            pltpu.VMEM((F, M, M, E), F32),
            pltpu.SemaphoreType.DMA((2, M)),
        ],
        compiler_params=pltpu.CompilerParams(vmem_limit_bytes=4 * 1024 * 1024),
    )(*kept)


def solution(mesh):
    in_specs = (
        P(None, None, None, "dev"),
        P("dev"),
        P("dev", None),
        P("dev", None),
        P(None, None, None, "dev"),
        P(None, "dev"),
        P("dev"),
        P(),
        P(None, "dev"),
        P(None, "dev"),
        P(None, "dev"),
        P(None, "dev"),
    )
    out_specs = (P(None, None, None, "dev"), P(None, None, None, "dev"))
    return jax.shard_map(
        functools.partial(shards, mesh.shape["dev"]),
        mesh=mesh,
        in_specs=in_specs,
        out_specs=out_specs,
        check_vma=False,
    )
```
